256 devices in a mesh: tm: 8 (over z), space: 32 (over y, x, core).
Axes of the slice: x: 4, y: 4, z: 8, core: 2. Of those that a mesh axis runs over, the one named last changes fastest.
Arguments:
- latent: bfloat16 [8, 64, 160, 384], P('tm', 'space'), may hold values from -6 to 6
- attn_gain: float32 [384], replicated, may hold values from 0.85 to 4.2
- qkv_weight: bfloat16 [384, 1152], replicated, may hold values from -1.5 to 1.5
- proj_weight: bfloat16 [384, 384], replicated, may hold values from -0.625 to 0.625
- conv_gain: float32 [384], replicated, may hold values from 0.25 to 1.75
- conv_weight: bfloat16 [3, 3, 3, 384, 384], replicated, may hold values from -0.0625 to 0.0625
- conv_bias: float32 [384], replicated, may hold values from -1.2 to 1.2
- time_weight: bfloat16 [3, 384, 768], replicated, may hold values from -0.1875 to 0.1875
- time_bias: float32 [768], replicated, may hold values from -1.2 to 1.2
- up_weight: bfloat16 [3, 3, 384, 192], replicated, may hold values from -0.109375 to 0.109375
- up_bias: float32 [192], replicated, may hold values from -1.2 to 1.2
Outputs:
- video: bfloat16 [16, 128, 320, 192], P('tm', 'space')
The draws below stay inside these ranges and needn't reach their ends.
All inputs are finite; a program needn't handle non-finite values.
Results may differ from the reference program's by a relative error of at most 0.015.
Values may be sent and summed in bfloat16 or wider, within the bound.
A program may use at most 128 MiB of HBM per device.

```python
import math
import jax
import jax.numpy as jnp
import numpy as np
from jax import lax

C = 384
C2 = 192
COLS = 160
FRAMES = 8
H = 64


def draw_attn_gain(key, part):
    key = jax.random.fold_in(key, 5)
    base = 1.0 + 0.15 * jax.random.uniform(key, (C,), jnp.float32, -1.0, 1.0)
    return base


def draw_latent(key, part):
    key = jax.random.fold_in(key, 7)
    keys = jax.random.split(key, 5)
    return jnp.clip(jax.random.normal(keys[4], (FRAMES, H, COLS, C), jnp.float32), -5.0, 5.0).astype(jnp.bfloat16)


def draw_qkv_weight(key, part):
    key = jax.random.fold_in(key, 11)
    noise = jax.random.normal(key, (C, 3 * C), jnp.float32) / jnp.sqrt(C * 1.0)
    row_ids = jnp.arange(C)[:, None]
    col_ids = jnp.arange(3 * C)[None, :]
    eye = (row_ids == col_ids % C).astype(jnp.float32)
    strength = 0.15
    spread = 1.6
    value = jnp.where(col_ids < 2 * C, strength * eye + spread * noise, noise)
    return jnp.clip(value, -1.5, 1.5).astype(jnp.bfloat16)


def centred(own_key, extent, scale, reach, kind=jnp.bfloat16):
    drawn = scale * jax.random.normal(own_key, extent, jnp.float32)
    return jnp.clip(drawn, min=-reach, max=reach).astype(kind)


def setup_inputs(seed: int = 0) -> dict:
    key_of = jax.random.split(jax.random.key(seed), 12)
    return {
        "latent": draw_latent(jax.random.fold_in(key_of[11], 71), 0),
        "attn_gain": draw_attn_gain(jax.random.fold_in(key_of[11], 71), 0),
        "qkv_weight": draw_qkv_weight(jax.random.fold_in(key_of[11], 71), 0),
        "proj_weight": centred(key_of[3], (C, C), (C // 4) ** -0.5, 0.625),
        "conv_gain": jnp.clip(1.0 + 0.15 * jax.random.normal(key_of[4], (C,), jnp.float32), 0.25, 1.75),
        "conv_weight": centred(key_of[5], (3, 3, 3, C, C), (27 * C) ** -0.5, 0.0625),
        "conv_bias": centred(key_of[6], (C,), 0.3, 1.2, jnp.float32),
        "time_weight": centred(key_of[7], (3, C, 2 * C), (3 * C) ** -0.5, 0.1875),
        "time_bias": centred(key_of[8], (2 * C,), 0.3, 1.2, jnp.float32),
        "up_weight": centred(key_of[9], (3, 3, C, C2), (9 * C) ** -0.5, 0.109375),
        "up_bias": centred(key_of[10], (C2,), 0.3, 1.2, jnp.float32),
    }


phase_table = np.array([[[1.0, 0.0, 0.0], [0.0, 1.0, 1.0]], [[1.0, 1.0, 0.0], [0.0, 0.0, 1.0]]], np.float32)

def rms(x, gain):
    values = x.astype(jnp.float32)
    return values * lax.rsqrt(lax.optimization_barrier(jnp.mean(values * values, axis=-1, keepdims=True)) + 1e-06) * gain

def phase_kernels(up_weight):
    table = jnp.asarray(phase_table).astype(jnp.float32)
    weight = up_weight.astype(jnp.float32)
    return jnp.einsum('aey,bfx,yxio->abefio', table, table, weight, precision=lax.Precision.HIGHEST).astype(jnp.bfloat16)

def phase_conv(coarse, kernels, bias, rows, cols):
    chans = coarse.shape[-1]
    outward = kernels.shape[-1]
    results = []
    for first in range(2):
        for second in range(2):
            taps = jnp.concatenate([coarse[:, first + e:first + e + rows, second + f:second + f + cols, :].reshape(-1, chans) for e in range(2) for f in range(2)], axis=1)
            value = jnp.dot(taps, kernels[first, second].reshape(4 * chans, outward), preferred_element_type=jnp.float32) + bias
            results.append(value.astype(jnp.bfloat16).reshape(-1, rows, cols, outward))
    stacked = jnp.stack(results, axis=0).reshape(2, 2, -1, rows, cols, outward)
    stacked = jnp.transpose(stacked, (2, 3, 0, 4, 1, 5))
    return stacked.reshape(-1, 2 * rows, 2 * cols, outward)

def reference(latent, attn_gain, qkv_weight, proj_weight, conv_gain, conv_weight, conv_bias, time_weight, time_bias, up_weight, up_bias):
    frames, rows, cols, chans = latent.shape
    count = rows * cols
    normed = rms(latent, attn_gain).astype(jnp.bfloat16)
    qkv = jnp.dot(normed.reshape(-1, chans), qkv_weight, preferred_element_type=jnp.float32).astype(jnp.bfloat16)
    qkv = qkv.reshape(frames, count, 3 * chans)
    block_rows = math.gcd(count, 1024)
    scale = 1.0 / math.sqrt(chans)

    def frame_attention(item):
        query = item[:, :chans]
        keys = item[:, chans:2 * chans]
        values = item[:, 2 * chans:]

        def one_block(rows_block):
            scores = jnp.dot(rows_block, keys.T, preferred_element_type=jnp.float32) * scale
            top = lax.optimization_barrier(jnp.max(scores, axis=1, keepdims=True))
            expo = jnp.exp(scores - top)
            total = lax.optimization_barrier(jnp.sum(expo, axis=1, keepdims=True))
            weights = expo.astype(jnp.bfloat16)
            summed = jnp.dot(weights, values, preferred_element_type=jnp.float32)
            return (summed / total).astype(jnp.bfloat16)
        return lax.map(one_block, query.reshape(count // block_rows, block_rows, chans)).reshape(count, chans)
    attn = lax.map(frame_attention, qkv)
    projected = jnp.dot(attn.reshape(-1, chans), proj_weight, preferred_element_type=jnp.float32)
    mid = (latent.astype(jnp.float32) + projected.reshape(latent.shape)).astype(jnp.bfloat16)
    act = jax.nn.silu(rms(mid, conv_gain)).astype(jnp.bfloat16)
    conv = lax.conv_general_dilated(act.astype(jnp.float32)[None], conv_weight.astype(jnp.float32), (1, 1, 1), ((2, 0), (1, 1), (1, 1)), dimension_numbers=('NDHWC', 'DHWIO', 'NDHWC'), precision=lax.Precision.HIGHEST)[0]
    block = (conv + conv_bias + mid.astype(jnp.float32)).astype(jnp.bfloat16)
    temporal = lax.conv_general_dilated(block.astype(jnp.float32)[None], time_weight.astype(jnp.float32).reshape(3, 1, 1, chans, 2 * chans), (1, 1, 1), ((2, 0), (0, 0), (0, 0)), dimension_numbers=('NDHWC', 'DHWIO', 'NDHWC'), precision=lax.Precision.HIGHEST)[0]
    doubled = (temporal + time_bias).astype(jnp.bfloat16)
    frames2 = jnp.stack([doubled[..., :chans], doubled[..., chans:]], axis=1).reshape(2 * frames, rows, cols, chans)
    kernels = phase_kernels(up_weight)

    def resample(frame):
        coarse = jnp.pad(frame, ((1, 1), (1, 1), (0, 0)))[None]
        return phase_conv(coarse, kernels, up_bias, rows, cols)[0]
    return lax.map(resample, frames2)
```

```python
import math

import jax
import jax.numpy as jnp
from jax import lax
from jax.experimental import pallas as pl
from jax.experimental.pallas import tpu as pltpu
from jax.sharding import PartitionSpec as P

MESH = pl.DeviceIdType.MESH
F32 = jnp.float32
BF16 = jnp.bfloat16
C = 384
COLS = 160
NT = (((1,), (1,)), ((), ()))


def rms(x, gain):
    values = x.astype(F32)
    return values * lax.rsqrt(jnp.mean(values * values, axis=-1, keepdims=True) + 1e-06) * gain


def silu(x):
    return x / (1.0 + jnp.exp(-x))


def dot(a, b):
    return jnp.dot(a, b, preferred_element_type=F32)


def flat(x):
    return x.reshape(-1, x.shape[-1])


def moved(x, steps):
    index = lax.broadcasted_iota(jnp.int32, x.shape, 0)
    edge = 0 if steps == 1 else COLS - 1
    rolled = pltpu.roll(x, steps % x.shape[0], 0)
    keep = index != edge
    for run in range(1, x.shape[0] // COLS):
        keep = keep & (index != edge + run * COLS)
    return jnp.where(keep, rolled, 0.0)


def kernel(
    latent, attn_gain, qkv_hbm, proj_hbm, conv_gain, conv_hbm, conv_bias, time_hbm, time_bias, up_hbm, up_bias,
    out,
    lat, nb, qb, acc, mx, den, acc_in, mx_in, den_in,
    qkv, proj, wc, wt, wu,
    mid, mid_in, act, conv, blocks, frames, wide,
    ss, rs, ws,
):
    z = lax.axis_index("tm")
    s = lax.axis_index("space")
    core = lax.rem(s, 2)
    x = lax.rem(s // 2, 4)
    y = s // 8
    pos1 = x + core * (y - x)
    pos2 = y + core * (x - y)
    step1 = 2 + 6 * core
    step2 = 8 - 6 * core

    def at(zz, ss_):
        return (zz, ss_)

    sib = at(z, s + 1 - 2 * core)
    far = at(z, lax.rem(s + 2 * core + 31, 32))
    f_plus = at(z, s + (lax.rem(pos1 + 1, 4) - pos1) * step1)
    f_minus = at(z, s + (lax.rem(pos1 + 3, 4) - pos1) * step1)
    g_plus = at(z, s + (lax.rem(pos2 + 1, 4) - pos2) * step2)
    g_minus = at(z, s + (lax.rem(pos2 + 3, 4) - pos2) * step2)
    z_plus = at(lax.rem(z + 1, 8), s)
    z_minus = at(lax.rem(z + 7, 8), s)
    z_plus2 = at(lax.rem(z + 2, 8), s)
    z_minus2 = at(lax.rem(z + 6, 8), s)
    s_up = at(z, lax.rem(s + 31, 32))
    s_down = at(z, lax.rem(s + 1, 32))

    pending = []
    local = []

    def send(src, dst, device):
        k = len(pending)
        copy = pltpu.make_async_remote_copy(
            src_ref=src, dst_ref=dst, send_sem=ss.at[k], recv_sem=rs.at[k], device_id=device, device_id_type=MESH
        )
        copy.start()
        pending.append(copy)
        return copy

    def load(src, dst):
        copy = pltpu.make_async_copy(src, dst, ws.at[len(local)])
        copy.start()
        local.append(copy)
        return copy

    barrier = pltpu.get_barrier_semaphore()
    partners = (sib, far, f_plus, f_minus, g_plus, g_minus, z_plus, z_minus, z_plus2, z_minus2)
    for partner in partners:
        pl.semaphore_signal(barrier, inc=1, device_id=partner, device_id_type=MESH)
    qkv_load = load(qkv_hbm, qkv)
    pl.semaphore_wait(barrier, len(partners))

    shift = [send(latent.at[0, r], lat.at[r], z_plus2) for r in range(2)]
    proj_load = load(proj_hbm, proj)
    conv_loads = [
        [load(conv_hbm.at[dt, :, dx], wc.at[dt, :, :, pl.ds(dx * C, C)]) for dx in range(3)] for dt in range(3)
    ]
    time_load = load(time_hbm, wt)
    up_load = load(up_hbm, wu)

    mx[...] = jnp.full(mx.shape, -1e30, F32)
    den[...] = jnp.zeros(den.shape, F32)
    acc[...] = jnp.zeros(acc.shape, F32)

    fp, fm, op, g, go = {}, {}, {}, {}, {}

    def along_second(r, i):
        g[r, i] = (send(nb.at[r, 0, i], nb.at[r, 3, i], g_plus), send(nb.at[r, 0, i], nb.at[r, 1, i], g_minus))

    def own(r):
        shift[r].wait_recv()
        nb[r, 0, 0] = rms(lat[r], attn_gain[...]).astype(BF16)
        fp[r] = send(nb.at[r, 0, 0], nb.at[r, 0, 3], f_plus)
        fm[r] = send(nb.at[r, 0, 0], nb.at[r, 0, 1], f_minus)
        along_second(r, 0)

    def first_axis(r):
        fp[r].wait_recv()
        if r == 0:
            op[r] = send(nb.at[r, 0, 3], nb.at[r, 0, 2], f_plus)
        along_second(r, 3)
        fm[r].wait_recv()
        if r == 1:
            op[r] = send(nb.at[r, 0, 1], nb.at[r, 0, 2], f_minus)
        along_second(r, 1)
        op[r].wait_recv()
        along_second(r, 2)

    def second_axis(r):
        for i in (0, 3, 1, 2):
            plus, minus = g[r, i]
            plus.wait_recv()
            if (r + i) % 2 == 0:
                go[r, i] = send(nb.at[r, 3, i], nb.at[r, 2, i], g_plus)
            minus.wait_recv()
            if (r + i) % 2 == 1:
                go[r, i] = send(nb.at[r, 1, i], nb.at[r, 2, i], g_minus)

    def last(r):
        for i in (0, 3, 1, 2):
            go[r, i].wait_recv()

    def attend(r, j, tiles=(0, 4)):
        def tile(t, carry):
            keys = flat(nb[r, j])
            scores = lax.dot_general(qb[t], keys, NT, preferred_element_type=F32)
            top = mx[t]
            new_top = jnp.maximum(top, jnp.max(scores, axis=1, keepdims=True))
            expo = jnp.exp2(scores - new_top[:, :1])
            fade = jnp.exp2(top - new_top)
            mx[t] = new_top
            den[t] = den[t] * fade + jnp.sum(expo, axis=1, keepdims=True)
            acc[t] = acc[t] * fade[:, :1] + dot(expo.astype(BF16), keys)
            return carry

        lax.fori_loop(tiles[0], tiles[1], tile, 0)

    own(0)
    first_axis(0)
    own(1)
    qkv_load.wait()
    scale = math.log2(math.e) / math.sqrt(C)
    normed = jnp.concatenate([nb[0, 0, 0], nb[1, 0, 0]], axis=0)
    query = dot(normed, qkv[:, :C]).astype(BF16)
    query = lax.dot_general(query, qkv[:, C : 2 * C], NT, preferred_element_type=F32) * scale
    qb[0:2] = query.astype(BF16).reshape(2, COLS, C)
    q_copy = send(qb.at[0:2], qb.at[2:4], sib)
    second_axis(0)
    first_axis(1)
    q_copy.wait_recv()
    attend(0, 0)
    attend(0, 3)
    attend(0, 1)
    second_axis(1)
    last(0)
    attend(0, 2)
    attend(1, 0)
    attend(1, 3)
    attend(1, 1)
    last(1)
    attend(1, 2, (2, 4))
    back = [
        send(acc.at[2:4], acc_in, sib),
        send(mx.at[2:4], mx_in, sib),
        send(den.at[2:4], den_in, sib),
    ]
    attend(1, 2, (0, 2))
    proj_load.wait()
    for copy in back:
        copy.wait_recv()
    top = jnp.maximum(mx[0:2], mx_in[...])
    mine = jnp.exp2(mx[0:2] - top)
    other = jnp.exp2(mx_in[...] - top)
    total = den[0:2] * mine + den_in[...] * other
    mine = (mine / total)[:, :, :1]
    other = (other / total)[:, :, :1]
    pooled = flat(acc[0:2] * mine + acc_in[...] * other).astype(BF16)
    attn = dot(pooled, qkv[:, 2 * C :]).astype(BF16)
    value = (flat(lat[...]).astype(F32) + dot(attn, proj[...])).astype(BF16)
    mid[...] = value.reshape(2, COLS, C)
    act[1, 1:3] = silu(rms(value, conv_gain[...])).astype(BF16).reshape(2, COLS, C)

    to_next = send(act.at[1, 1:3], act.at[0, 1:3], z_plus)
    to_previous = send(mid, mid_in, z_minus)

    def edges(f):
        return [send(act.at[f, 1], act.at[f, 3], s_up), send(act.at[f, 2], act.at[f, 0], s_down)]

    def settle(copies, f):
        for copy in copies:
            copy.wait_recv()

        @pl.when(s == 0)
        def _():
            act[f, 0] = jnp.zeros((COLS, C), BF16)

        @pl.when(s == 31)
        def _():
            act[f, 3] = jnp.zeros((COLS, C), BF16)

    def convolve(f):
        taps = jnp.concatenate([flat(act[f, dy : dy + 2]) for dy in range(3)], axis=1)
        conv[...] += dot(taps, wc[f].reshape(3 * C, 3 * C))

    halo = {1: edges(1)}
    conv[...] = jnp.zeros(conv.shape, F32)
    for row in conv_loads:
        for copy in row:
            copy.wait()
    settle(halo[1], 1)

    @pl.when(z != 1)
    def _():
        convolve(1)

    to_next.wait_recv()
    halo[0] = edges(0)
    to_previous.wait_recv()
    act[2, 1:3] = silu(rms(flat(mid_in[...]), conv_gain[...])).astype(BF16).reshape(2, COLS, C)
    halo[2] = edges(2)
    settle(halo[0], 0)

    @pl.when((z != 1) & (z != 2))
    def _():
        convolve(0)

    settle(halo[2], 2)
    convolve(2)
    value = conv[:, C : 2 * C] + moved(conv[:, :C], 1) + moved(conv[:, 2 * C :], -1)
    value = (value + conv_bias[...] + flat(mid_in[...]).astype(F32)).astype(BF16)
    blocks[1] = value
    next_block = send(blocks.at[1], blocks.at[0], z_plus)
    previous_block = send(blocks.at[1], blocks.at[2], z_minus)
    time_load.wait()
    total = dot(jnp.where(z >= 1, value, jnp.zeros_like(value)), wt[1]) + time_bias[...]
    next_block.wait_recv()
    total += dot(jnp.where(z >= 2, blocks[0], jnp.zeros_like(value)), wt[0])
    previous_block.wait_recv()
    total += dot(blocks[2], wt[2])
    doubled = total.astype(BF16).reshape(2, COLS, 2 * C)
    frames[1:3, 0] = doubled[:, :, :C]
    frames[1:3, 1] = doubled[:, :, C:]
    above = send(frames.at[1], frames.at[3], s_up)
    below = send(frames.at[2], frames.at[0], s_down)
    up_load.wait()

    def upsample(i, a):
        taps = jnp.concatenate([flat(frames[i + a]), flat(frames[i + a + 1])], axis=1)
        value = dot(taps, wu[a])
        side = value[:, C:]
        lane = lax.broadcasted_iota(jnp.int32, side.shape, 1)
        value = value[:, :C] + jnp.where(lane < C // 2, moved(side, 1), moved(side, -1)) + up_bias[...]
        second = pltpu.roll(value, C // 2, 1)
        for frame in range(2):
            rows = slice(frame * COLS, (frame + 1) * COLS)
            for part in range(2):
                lanes = slice(128 * part, 128 * part + 128)
                wide[part, pl.ds(0, COLS, stride=2), :] = value[rows, lanes]
                wide[part, pl.ds(1, COLS, stride=2), :] = second[rows, lanes]
            out[frame, 2 * i + a, :, :128] = wide[0].astype(BF16)
            out[frame, 2 * i + a, :, 128:] = wide[1, :, : C // 2 - 128].astype(BF16)

    upsample(0, 1)
    upsample(1, 0)
    above.wait_recv()
    below.wait_recv()

    @pl.when(s == 0)
    def _():
        frames[0] = jnp.zeros((2, COLS, C), BF16)

    @pl.when(s == 31)
    def _():
        frames[3] = jnp.zeros((2, COLS, C), BF16)

    upsample(0, 0)
    upsample(1, 1)
    for copy in pending:
        copy.wait_send()


def up_table(up_weight):
    weight = up_weight.astype(F32)
    rows = [[weight[0], weight[1] + weight[2]], [weight[0] + weight[1], weight[2]]]

    def cell(a, b, e, f):
        row = rows[a][e]
        return [[row[0], row[1] + row[2]], [row[0] + row[1], row[2]]][b][f].astype(BF16)

    return jnp.stack(
        [
            jnp.concatenate(
                [
                    jnp.concatenate([cell(a, b, e, f) for b, f in ((0, 1), (1, 0), (0, 0), (1, 1))], axis=1)
                    for e in range(2)
                ],
                axis=0,
            )
            for a in range(2)
        ]
    )


SENDS = 64
LOADS = 16


def body(
    latent, attn_gain, qkv_weight, proj_weight, conv_gain, conv_weight, conv_bias, time_weight, time_bias, up_weight,
    up_bias,
):
    table = up_table(up_weight)
    bias2 = jnp.concatenate([up_bias, up_bias])
    vmem = pl.BlockSpec(memory_space=pltpu.VMEM)
    anywhere = pl.BlockSpec(memory_space=pl.ANY)
    return pl.pallas_call(
        kernel,
        out_shape=jax.ShapeDtypeStruct((2, 4, 2 * COLS, C // 2), BF16),
        in_specs=[
            anywhere, vmem, anywhere, anywhere, vmem, anywhere, vmem, anywhere, vmem, anywhere, vmem,
        ],
        out_specs=vmem,
        scratch_shapes=[
            pltpu.VMEM((2, COLS, C), BF16),
            pltpu.VMEM((2, 4, 4, COLS, C), BF16),
            pltpu.VMEM((4, COLS, C), BF16),
            pltpu.VMEM((4, COLS, C), F32),
            pltpu.VMEM((4, COLS, 128), F32),
            pltpu.VMEM((4, COLS, 128), F32),
            pltpu.VMEM((2, COLS, C), F32),
            pltpu.VMEM((2, COLS, 128), F32),
            pltpu.VMEM((2, COLS, 128), F32),
            pltpu.VMEM((C, 3 * C), BF16),
            pltpu.VMEM((C, C), BF16),
            pltpu.VMEM((3, 3, C, 3 * C), BF16),
            pltpu.VMEM((3, C, 2 * C), BF16),
            pltpu.VMEM((2, 2 * C, 2 * C), BF16),
            pltpu.VMEM((2, COLS, C), BF16),
            pltpu.VMEM((2, COLS, C), BF16),
            pltpu.VMEM((3, 4, COLS, C), BF16),
            pltpu.VMEM((2 * COLS, 3 * C), F32),
            pltpu.VMEM((3, 2 * COLS, C), BF16),
            pltpu.VMEM((4, 2, COLS, C), BF16),
            pltpu.VMEM((2, 2 * COLS, 128), F32),
            pltpu.SemaphoreType.DMA((SENDS,)),
            pltpu.SemaphoreType.DMA((SENDS,)),
            pltpu.SemaphoreType.DMA((LOADS,)),
        ],
        compiler_params=pltpu.CompilerParams(
            collective_id=0, has_side_effects=True, vmem_limit_bytes=56 * 1024 * 1024
        ),
    )(
        latent, attn_gain[None], qkv_weight, proj_weight, conv_gain[None], conv_weight, conv_bias[None], time_weight,
        time_bias[None], table, bias2[None],
    )


def solution(mesh):
    return jax.shard_map(
        body,
        mesh=mesh,
        in_specs=(P("tm", "space", None, None), P(), P(), P(), P(), P(), P(), P(), P(), P(), P()),
        out_specs=P("tm", "space", None, None),
        check_vma=False,
    )
```

```python
import math

import jax
import jax.numpy as jnp
from jax import lax
from jax.experimental import pallas as pl
from jax.experimental.pallas import tpu as pltpu
from jax.sharding import PartitionSpec as P

MESH = pl.DeviceIdType.MESH
F32 = jnp.float32
BF16 = jnp.bfloat16
C = 384
COLS = 160
NT = (((1,), (1,)), ((), ()))
PARTS = 4
PART = 80
OWN = PARTS * PART
SIDES = (0, 3, 1, 2)
ORDER = (
    ("own", 0), ("own", 1), ("f+", 0), ("f-", 0), ("g+", 0, 0), ("g-", 0, 0), ("own", 2), ("f-", 1), ("g-", 1, 0),
    ("g-", 0, 3), ("g-", 0, 1), ("f+", 1), ("g+", 1, 0), ("own", 3), ("f-", 2), ("g-", 2, 0), ("g+", 0, 3),
    ("op", 0), ("g+", 0, 1), ("go", 0, 0), ("query", 0), ("f+", 2), ("g+", 2, 0), ("attend", 0, 0, 1), ("g+", 1, 1),
    ("g-", 1, 1), ("op", 1), ("g+", 1, 3), ("go", 1, 0), ("go", 0, 3), ("go", 0, 1), ("f+", 3), ("g+", 3, 0),
    ("g+", 2, 1), ("g+", 0, 2), ("g-", 1, 3), ("f-", 3), ("g-", 3, 0), ("g-", 2, 1), ("g-", 0, 2),
    ("attend", 0, 1, 2), ("table", 0), ("g-", 2, 3), ("g-", 1, 2), ("g+", 2, 3), ("op", 2), ("go", 2, 0),
    ("g-", 3, 3), ("go", 1, 1), ("g+", 1, 2), ("attend", 1, 1, 2), ("go", 1, 3), ("g+", 3, 3), ("go", 0, 2),
    ("g+", 3, 1), ("g+", 2, 2), ("g-", 3, 1), ("op", 3), ("go", 3, 0), ("go", 2, 1), ("attend", 0, 3, 2),
    ("go", 2, 3), ("go", 1, 2), ("g-", 2, 2), ("attend", 1, 3, 2), ("g-", 3, 2), ("attend", 2, 1, 2), ("go", 3, 3),
    ("go", 3, 1), ("go", 2, 2), ("g+", 3, 2), ("attend", 2, 3, 2), ("go", 3, 2), ("attend", 3, 1, 2),
)


def rms(x, gain):
    values = x.astype(F32)
    return values * lax.rsqrt(jnp.mean(values * values, axis=-1, keepdims=True) + 1e-06) * gain


def silu(x):
    return x / (1.0 + jnp.exp(-x))


def dot(a, b):
    return jnp.dot(a, b, preferred_element_type=F32)


def flat(x):
    return x.reshape(-1, x.shape[-1])


def moved(x, steps):
    index = lax.broadcasted_iota(jnp.int32, x.shape, 0)
    edge = 0 if steps == 1 else COLS - 1
    rolled = pltpu.roll(x, steps % x.shape[0], 0)
    keep = index != edge
    for run in range(1, x.shape[0] // COLS):
        keep = keep & (index != edge + run * COLS)
    return jnp.where(keep, rolled, 0.0)


def kernel(
    latent, attn_gain, qkv_hbm, proj_hbm, conv_gain, conv_hbm, conv_bias, time_hbm, time_bias, up_hbm, up_bias,
    out,
    lat, nb, qb, acc, mx, den, acc_in, mx_in, den_in,
    qkv, proj, wc, wt, up, wu,
    mid, mid_in, act, conv, blocks, frames, wide,
    ss, rs, ws,
):
    z = lax.axis_index("tm")
    s = lax.axis_index("space")
    core = lax.rem(s, 2)
    x = lax.rem(s // 2, 4)
    y = s // 8
    pos1 = x + core * (y - x)
    pos2 = y + core * (x - y)
    step1 = 2 + 6 * core
    step2 = 8 - 6 * core

    def at(zz, ss_):
        return (zz, ss_)

    sib = at(z, s + 1 - 2 * core)
    far = at(z, lax.rem(s + 2 * core + 31, 32))
    f_plus = at(z, s + (lax.rem(pos1 + 1, 4) - pos1) * step1)
    f_minus = at(z, s + (lax.rem(pos1 + 3, 4) - pos1) * step1)
    g_plus = at(z, s + (lax.rem(pos2 + 1, 4) - pos2) * step2)
    g_minus = at(z, s + (lax.rem(pos2 + 3, 4) - pos2) * step2)
    z_plus = at(lax.rem(z + 1, 8), s)
    z_minus = at(lax.rem(z + 7, 8), s)
    z_plus2 = at(lax.rem(z + 2, 8), s)
    z_minus2 = at(lax.rem(z + 6, 8), s)
    s_up = at(z, lax.rem(s + 31, 32))
    s_down = at(z, lax.rem(s + 1, 32))

    pending = []
    local = []

    def send(src, dst, device):
        k = len(pending)
        copy = pltpu.make_async_remote_copy(
            src_ref=src, dst_ref=dst, send_sem=ss.at[k], recv_sem=rs.at[k], device_id=device, device_id_type=MESH
        )
        copy.start()
        pending.append(copy)
        return copy


    def load(src, dst):
        copy = pltpu.make_async_copy(src, dst, ws.at[len(local)])
        copy.start()
        local.append(copy)
        return copy

    barrier = pltpu.get_barrier_semaphore()
    partners = (sib, far, f_plus, f_minus, g_plus, g_minus, z_plus, z_minus, z_plus2, z_minus2)
    for partner in partners:
        pl.semaphore_signal(barrier, inc=1, device_id=partner, device_id_type=MESH)
    qkv_load = load(qkv_hbm, qkv)
    pl.semaphore_wait(barrier, len(partners))

    shift = [
        send(latent.at[0, c // 2, pl.ds(c % 2 * PART, PART)], lat.at[c], z_plus2) for c in range(PARTS)
    ]
    proj_load = load(proj_hbm, proj)
    conv_loads = [
        [load(conv_hbm.at[dt, :, dx], wc.at[dt, :, :, pl.ds(dx * C, C)]) for dx in range(3)] for dt in range(3)
    ]
    time_load = load(time_hbm, wt)
    up_load = load(up_hbm, up)

    mx[...] = jnp.full(mx.shape, -1e30, F32)
    den[...] = jnp.zeros(den.shape, F32)
    acc[...] = jnp.zeros(acc.shape, F32)

    copies = {}

    def slot(c, j, i):
        return nb.at[4 * c + SIDES.index(j), i]

    def along_second(c, i):
        copies["g+", c, i] = send(slot(c, 0, i), slot(c, 3, i), g_plus)
        copies["g-", c, i] = send(slot(c, 0, i), slot(c, 1, i), g_minus)

    def step(kind, c, i=0):
        if kind == "own":
            shift[c].wait_recv()
            nb[4 * c, 0] = rms(lat[c], attn_gain[...].reshape(1, C)).astype(BF16)
            copies["f+", c, 0] = send(slot(c, 0, 0), slot(c, 0, 3), f_plus)
            copies["f-", c, 0] = send(slot(c, 0, 0), slot(c, 0, 1), f_minus)
            along_second(c, 0)
            return
        copies[kind, c, i].wait_recv()
        if kind == "f+":
            if c % 2 == 0:
                copies["op", c, 0] = send(slot(c, 0, 3), slot(c, 0, 2), f_plus)
            along_second(c, 3)
        elif kind == "f-":
            if c % 2 == 1:
                copies["op", c, 0] = send(slot(c, 0, 1), slot(c, 0, 2), f_minus)
            along_second(c, 1)
        elif kind == "op":
            along_second(c, 2)
        elif kind == "g+" and (c + i) % 2 == 0:
            copies["go", c, i] = send(slot(c, 3, i), slot(c, 2, i), g_plus)
        elif kind == "g-" and (c + i) % 2 == 1:
            copies["go", c, i] = send(slot(c, 1, i), slot(c, 2, i), g_minus)

    def project():
        qkv_load.wait()
        scale = math.log2(math.e) / math.sqrt(C)
        normed = jnp.concatenate([nb[4 * c, 0] for c in range(PARTS)], axis=0)
        query = dot(normed, qkv[:, :C]).astype(BF16)
        query = lax.dot_general(query, qkv[:, C : 2 * C], NT, preferred_element_type=F32) * scale
        qb[:OWN] = query.astype(BF16)
        return send(qb.at[pl.ds(0, OWN)], qb.at[pl.ds(OWN, OWN)], sib)

    def attend(c, p, n, low=0, size=2 * OWN):
        rows = slice(low, low + size)
        count = n * OWN
        keys = nb[4 * c + p : 4 * c + p + n].reshape(count, C)
        scores = lax.dot_general(qb[rows], keys, NT, preferred_element_type=F32)
        top = mx[rows]
        new_top = jnp.maximum(top, jnp.max(scores, axis=1, keepdims=True))
        expo = jnp.exp2(scores - jnp.tile(new_top, (1, -(-count // 128)))[:, :count])
        fade = jnp.exp2(top - new_top)
        if count % 128 == 0:
            part = expo[:, :128]
            for lane in range(128, count, 128):
                part = part + expo[:, lane : lane + 128]
        else:
            part = jnp.sum(expo, axis=1, keepdims=True) * (1.0 / 128.0)
        mx[rows] = new_top
        den[rows] = den[rows] * fade + part
        acc[rows] = acc[rows] * jnp.tile(fade, (1, C // 128)) + dot(expo.astype(BF16), keys)

    def table():
        def summed(parts):
            return parts[0] if len(parts) == 1 else parts[0] + parts[1]

        spans = {(0, 0): (0,), (0, 1): (1, 2), (1, 0): (0, 1), (1, 1): (2,)}
        for a in range(2):
            for e in range(2):
                rows = [summed([up[dy, dx].astype(F32) for dy in spans[a, e]]) for dx in range(3)]
                for k, (b, f) in enumerate(((0, 1), (1, 0), (0, 0), (1, 1))):
                    cell = summed([rows[dx] for dx in spans[b, f]]).astype(BF16)
                    wu[a, k * C // 2 : (k + 1) * C // 2, e * C : (e + 1) * C] = cell

    for kind, c, *rest in ORDER:
        if kind == "query":
            q_copy = project()
        elif kind == "attend":
            attend(c, *rest)
        elif kind == "table":
            up_load.wait()
            table()
        else:
            step(kind, c, *rest)
            if (kind, c) == ("g+", 2) and rest == [0]:
                q_copy.wait_recv()
    attend(PARTS - 1, 3, 1, OWN, OWN)
    back = [
        send(acc.at[pl.ds(OWN, OWN)], acc_in, sib),
        send(mx.at[pl.ds(OWN, OWN)], mx_in, sib),
        send(den.at[pl.ds(OWN, OWN)], den_in, sib),
    ]
    attend(PARTS - 1, 3, 1, 0, OWN)
    proj_load.wait()
    for copy in back:
        copy.wait_recv()
    top = jnp.maximum(mx[:OWN], mx_in[...])
    mine = jnp.exp2(mx[:OWN] - top)
    other = jnp.exp2(mx_in[...] - top)
    total = jnp.sum(den[:OWN] * mine + den_in[...] * other, axis=1, keepdims=True)
    mine = jnp.tile(mine / total, (1, C // 128))
    other = jnp.tile(other / total, (1, C // 128))
    pooled = (acc[:OWN] * mine + acc_in[...] * other).astype(BF16)
    attn = dot(pooled, qkv[:, 2 * C :]).astype(BF16)
    value = (flat(lat[...]).astype(F32) + dot(attn, proj[...])).astype(BF16)
    mid[...] = value.reshape(2, COLS, C)
    act[1, 1:3] = silu(rms(value, conv_gain[...].reshape(1, C))).astype(BF16).reshape(2, COLS, C)


    to_next = send(act.at[1, 1:3], act.at[0, 1:3], z_plus)
    to_previous = send(mid, mid_in, z_minus)

    def edges(f):
        return [send(act.at[f, 1], act.at[f, 3], s_up), send(act.at[f, 2], act.at[f, 0], s_down)]

    def settle(copies, f):
        for copy in copies:
            copy.wait_recv()

        @pl.when(s == 0)
        def _():
            act[f, 0] = jnp.zeros((COLS, C), BF16)

        @pl.when(s == 31)
        def _():
            act[f, 3] = jnp.zeros((COLS, C), BF16)

    def convolve(f):
        taps = jnp.concatenate([flat(act[f, dy : dy + 2]) for dy in range(3)], axis=1)
        conv[...] += dot(taps, wc[f].reshape(3 * C, 3 * C))

    halo = {1: edges(1)}
    conv[...] = jnp.zeros(conv.shape, F32)
    for row in conv_loads:
        for copy in row:
            copy.wait()
    settle(halo[1], 1)

    @pl.when(z != 1)
    def _():
        convolve(1)

    to_next.wait_recv()
    halo[0] = edges(0)
    to_previous.wait_recv()
    act[2, 1:3] = silu(rms(flat(mid_in[...]), conv_gain[...].reshape(1, C))).astype(BF16).reshape(2, COLS, C)
    halo[2] = edges(2)
    settle(halo[0], 0)

    @pl.when((z != 1) & (z != 2))
    def _():
        convolve(0)

    settle(halo[2], 2)
    convolve(2)
    value = conv[:, C : 2 * C] + moved(conv[:, :C], 1) + moved(conv[:, 2 * C :], -1)
    value = (value + conv_bias[...].reshape(1, C) + flat(mid_in[...]).astype(F32)).astype(BF16)
    blocks[1] = value
    next_block = send(blocks.at[1], blocks.at[0], z_plus)
    previous_block = send(blocks.at[1], blocks.at[2], z_minus)
    time_load.wait()
    total = dot(jnp.where(z >= 1, value, jnp.zeros_like(value)), wt[1]) + time_bias[...].reshape(1, 2 * C)
    next_block.wait_recv()
    total += dot(jnp.where(z >= 2, blocks[0], jnp.zeros_like(value)), wt[0])
    previous_block.wait_recv()
    total += dot(blocks[2], wt[2])
    doubled = total.astype(BF16).reshape(2, COLS, 2 * C)
    frames[1:3, 0] = doubled[:, :, :C]
    frames[1:3, 1] = doubled[:, :, C:]
    above = send(frames.at[1], frames.at[3], s_up)
    below = send(frames.at[2], frames.at[0], s_down)

    bias = up_bias[...].reshape(1, C // 2)

    def upsample(i, a):
        taps = jnp.concatenate([flat(frames[i + a]), flat(frames[i + a + 1])], axis=1)
        value = lax.dot_general(taps, wu[a], NT, preferred_element_type=F32)
        side = value[:, C:]
        lane = lax.broadcasted_iota(jnp.int32, side.shape, 1)
        value = value[:, :C] + jnp.where(lane < C // 2, moved(side, 1), moved(side, -1))
        second = pltpu.roll(value, C // 2, 1)
        for frame in range(2):
            rows = slice(frame * COLS, (frame + 1) * COLS)
            for part in range(2):
                lanes = slice(128 * part, 128 * part + 128)
                wide[part, pl.ds(0, COLS, stride=2), :] = value[rows, lanes]
                wide[part, pl.ds(1, COLS, stride=2), :] = second[rows, lanes]
            out[frame, 2 * i + a, :, :128] = (wide[0] + bias[:, :128]).astype(BF16)
            out[frame, 2 * i + a, :, 128:] = (wide[1, :, : C // 2 - 128] + bias[:, 128:]).astype(BF16)

    upsample(0, 1)
    upsample(1, 0)
    above.wait_recv()
    below.wait_recv()

    @pl.when(s == 0)
    def _():
        frames[0] = jnp.zeros((2, COLS, C), BF16)

    @pl.when(s == 31)
    def _():
        frames[3] = jnp.zeros((2, COLS, C), BF16)

    upsample(0, 0)
    upsample(1, 1)
    for copy in pending:
        copy.wait_send()


SENDS = 96
LOADS = 16


def body(
    latent, attn_gain, qkv_weight, proj_weight, conv_gain, conv_weight, conv_bias, time_weight, time_bias, up_weight,
    up_bias,
):
    vmem = pl.BlockSpec(memory_space=pltpu.VMEM)
    anywhere = pl.BlockSpec(memory_space=pl.ANY)
    return pl.pallas_call(
        kernel,
        out_shape=jax.ShapeDtypeStruct((2, 4, 2 * COLS, C // 2), BF16),
        in_specs=[
            anywhere, vmem, anywhere, anywhere, vmem, anywhere, vmem, anywhere, vmem, anywhere, vmem,
        ],
        out_specs=vmem,
        scratch_shapes=[
            pltpu.VMEM((PARTS, PART, C), BF16),
            pltpu.VMEM((4 * PARTS, 4, PART, C), BF16),
            pltpu.VMEM((2 * OWN, C), BF16),
            pltpu.VMEM((2 * OWN, C), F32),
            pltpu.VMEM((2 * OWN, 128), F32),
            pltpu.VMEM((2 * OWN, 128), F32),
            pltpu.VMEM((OWN, C), F32),
            pltpu.VMEM((OWN, 128), F32),
            pltpu.VMEM((OWN, 128), F32),
            pltpu.VMEM((C, 3 * C), BF16),
            pltpu.VMEM((C, C), BF16),
            pltpu.VMEM((3, 3, C, 3 * C), BF16),
            pltpu.VMEM((3, C, 2 * C), BF16),
            pltpu.VMEM((3, 3, C // 2, C), BF16),
            pltpu.VMEM((2, 2 * C, 2 * C), BF16),
            pltpu.VMEM((2, COLS, C), BF16),
            pltpu.VMEM((2, COLS, C), BF16),
            pltpu.VMEM((3, 4, COLS, C), BF16),
            pltpu.VMEM((2 * COLS, 3 * C), F32),
            pltpu.VMEM((3, 2 * COLS, C), BF16),
            pltpu.VMEM((4, 2, COLS, C), BF16),
            pltpu.VMEM((2, 2 * COLS, 128), F32),
            pltpu.SemaphoreType.DMA((SENDS,)),
            pltpu.SemaphoreType.DMA((SENDS,)),
            pltpu.SemaphoreType.DMA((LOADS,)),
        ],
        compiler_params=pltpu.CompilerParams(
            collective_id=0, has_side_effects=True, vmem_limit_bytes=56 * 1024 * 1024
        ),
    )(
        latent, attn_gain, qkv_weight, proj_weight, conv_gain, conv_weight, conv_bias, time_weight, time_bias,
        jnp.swapaxes(up_weight, 2, 3), up_bias,
    )


def solution(mesh):
    return jax.shard_map(
        body,
        mesh=mesh,
        in_specs=(P("tm", "space", None, None), P(), P(), P(), P(), P(), P(), P(), P(), P(), P()),
        out_specs=P("tm", "space", None, None),
        check_vma=False,
    )
```

```python
import math

import jax
import jax.numpy as jnp
from jax import lax
from jax.experimental import pallas as pl
from jax.experimental.pallas import tpu as pltpu
from jax.sharding import PartitionSpec as P

MESH = pl.DeviceIdType.MESH
F32 = jnp.float32
BF16 = jnp.bfloat16
C = 384
COLS = 160
NT = (((1,), (1,)), ((), ()))
PARTS = 4
PART = 80
OWN = PARTS * PART
SIDES = (0, 3, 1, 2)
TIMES = (0, 2, 1)
ORDER = (
    ("own", 0), ("own", 1), ("f+", 0), ("f-", 0), ("g+", 0, 0), ("g-", 0, 0), ("own", 2), ("f-", 1), ("g-", 1, 0),
    ("g-", 0, 3), ("g-", 0, 1), ("f+", 1), ("g+", 1, 0), ("own", 3), ("f-", 2), ("g-", 2, 0), ("g+", 0, 3),
    ("op", 0), ("g+", 0, 1), ("go", 0, 0), ("query", 0), ("f+", 2), ("g+", 2, 0), ("attend", 0, 0, 1), ("g+", 1, 1),
    ("g-", 1, 1), ("op", 1), ("g+", 1, 3), ("go", 1, 0), ("go", 0, 3), ("go", 0, 1), ("f+", 3), ("g+", 3, 0),
    ("g+", 2, 1), ("g+", 0, 2), ("g-", 1, 3), ("f-", 3), ("g-", 3, 0), ("g-", 2, 1), ("g-", 0, 2),
    ("attend", 0, 1, 2), ("table", 0), ("g-", 2, 3), ("g-", 1, 2), ("g+", 2, 3), ("op", 2), ("go", 2, 0),
    ("g-", 3, 3), ("go", 1, 1), ("g+", 1, 2), ("attend", 1, 1, 2), ("go", 1, 3), ("g+", 3, 3), ("go", 0, 2),
    ("g+", 3, 1), ("g+", 2, 2), ("g-", 3, 1), ("op", 3), ("go", 3, 0), ("go", 2, 1), ("attend", 0, 3, 2),
    ("go", 2, 3), ("go", 1, 2), ("g-", 2, 2), ("attend", 1, 3, 2), ("g-", 3, 2), ("attend", 2, 1, 2), ("go", 3, 3),
    ("go", 3, 1), ("go", 2, 2), ("g+", 3, 2), ("attend", 2, 3, 2), ("go", 3, 2), ("attend", 3, 1, 2),
)


def rms(x, gain):
    values = x.astype(F32)
    return values * lax.rsqrt(jnp.mean(values * values, axis=-1, keepdims=True) + 1e-06) * gain


def silu(x):
    return x / (1.0 + jnp.exp(-x))


def dot(a, b):
    return jnp.dot(a, b, preferred_element_type=F32)


def flat(x):
    return x.reshape(-1, x.shape[-1])


def moved(x, steps):
    index = lax.broadcasted_iota(jnp.int32, x.shape, 0)
    edge = 0 if steps == 1 else COLS - 1
    rolled = pltpu.roll(x, steps % x.shape[0], 0)
    keep = index != edge
    for run in range(1, x.shape[0] // COLS):
        keep = keep & (index != edge + run * COLS)
    return jnp.where(keep, rolled, 0.0)


def kernel(
    latent, attn_gain, qkv_hbm, proj_hbm, conv_gain, conv_hbm, conv_bias, time_hbm, time_bias, up_hbm, up_bias,
    out,
    lat, nb, qb, acc, mx, den, acc_in, mx_in, den_in,
    qkv, proj, wc, wt, up, wu,
    mid, mid_in, act, conv, blocks, frames, wide,
    ss, rs, ws,
):
    z = lax.axis_index("tm")
    s = lax.axis_index("space")
    core = lax.rem(s, 2)
    x = lax.rem(s // 2, 4)
    y = s // 8
    pos1 = x + core * (y - x)
    pos2 = y + core * (x - y)
    step1 = 2 + 6 * core
    step2 = 8 - 6 * core

    def at(zz, ss_):
        return (zz, ss_)

    sib = at(z, s + 1 - 2 * core)
    far = at(z, lax.rem(s + 2 * core + 31, 32))
    f_plus = at(z, s + (lax.rem(pos1 + 1, 4) - pos1) * step1)
    f_minus = at(z, s + (lax.rem(pos1 + 3, 4) - pos1) * step1)
    g_plus = at(z, s + (lax.rem(pos2 + 1, 4) - pos2) * step2)
    g_minus = at(z, s + (lax.rem(pos2 + 3, 4) - pos2) * step2)
    z_plus = at(lax.rem(z + 1, 8), s)
    z_minus = at(lax.rem(z + 7, 8), s)
    z_plus2 = at(lax.rem(z + 2, 8), s)
    z_minus2 = at(lax.rem(z + 6, 8), s)

    pending = []
    local = []

    def send(src, dst, device):
        k = len(pending)
        copy = pltpu.make_async_remote_copy(
            src_ref=src, dst_ref=dst, send_sem=ss.at[k], recv_sem=rs.at[k], device_id=device, device_id_type=MESH
        )
        copy.start()
        pending.append(copy)
        return copy


    def load(src, dst):
        copy = pltpu.make_async_copy(src, dst, ws.at[len(local)])
        copy.start()
        local.append(copy)
        return copy

    barrier = pltpu.get_barrier_semaphore()
    partners = (sib, far, f_plus, f_minus, g_plus, g_minus, z_plus, z_minus, z_plus2, z_minus2)
    for partner in partners:
        pl.semaphore_signal(barrier, inc=1, device_id=partner, device_id_type=MESH)
    qkv_load = load(qkv_hbm, qkv)
    pl.semaphore_wait(barrier, len(partners))

    shift = [
        send(latent.at[0, c // 2, pl.ds(c % 2 * PART, PART)], lat.at[c], z_plus2) for c in range(PARTS)
    ]
    proj_load = load(proj_hbm, proj)
    conv_loads = [
        [load(conv_hbm.at[dt, :, dx], wc.at[TIMES.index(dt), :, :, pl.ds(dx * C, C)]) for dx in range(3)]
        for dt in TIMES
    ]
    time_loads = [load(time_hbm.at[dt], wt.at[TIMES.index(dt)]) for dt in TIMES]
    up_load = load(up_hbm, up)

    mx[...] = jnp.full(mx.shape, -1e30, F32)
    den[...] = jnp.zeros(den.shape, F32)
    acc[...] = jnp.zeros(acc.shape, F32)

    copies = {}

    def slot(c, j, i):
        return nb.at[4 * c + SIDES.index(j), i]

    def along_second(c, i):
        copies["g+", c, i] = send(slot(c, 0, i), slot(c, 3, i), g_plus)
        copies["g-", c, i] = send(slot(c, 0, i), slot(c, 1, i), g_minus)

    def step(kind, c, i=0):
        if kind == "own":
            shift[c].wait_recv()
            nb[4 * c, 0] = rms(lat[c], attn_gain[...].reshape(1, C)).astype(BF16)
            copies["f+", c, 0] = send(slot(c, 0, 0), slot(c, 0, 3), f_plus)
            copies["f-", c, 0] = send(slot(c, 0, 0), slot(c, 0, 1), f_minus)
            along_second(c, 0)
            return
        copies[kind, c, i].wait_recv()
        if kind == "f+":
            if c % 2 == 0:
                copies["op", c, 0] = send(slot(c, 0, 3), slot(c, 0, 2), f_plus)
            along_second(c, 3)
        elif kind == "f-":
            if c % 2 == 1:
                copies["op", c, 0] = send(slot(c, 0, 1), slot(c, 0, 2), f_minus)
            along_second(c, 1)
        elif kind == "op":
            along_second(c, 2)
        elif kind == "g+" and (c + i) % 2 == 0:
            copies["go", c, i] = send(slot(c, 3, i), slot(c, 2, i), g_plus)
        elif kind == "g-" and (c + i) % 2 == 1:
            copies["go", c, i] = send(slot(c, 1, i), slot(c, 2, i), g_minus)

    def project():
        qkv_load.wait()
        scale = math.log2(math.e) / math.sqrt(C)
        normed = jnp.concatenate([nb[4 * c, 0] for c in range(PARTS)], axis=0)
        query = dot(normed, qkv[:, :C]).astype(BF16)
        query = lax.dot_general(query, qkv[:, C : 2 * C], NT, preferred_element_type=F32) * scale
        qb[:OWN] = query.astype(BF16)
        return send(qb.at[pl.ds(0, OWN)], qb.at[pl.ds(OWN, OWN)], sib)

    def attend(c, p, n, low=0, size=2 * OWN):
        rows = slice(low, low + size)
        count = n * OWN
        keys = nb[4 * c + p : 4 * c + p + n].reshape(count, C)
        scores = lax.dot_general(qb[rows], keys, NT, preferred_element_type=F32)
        top = mx[rows]
        new_top = jnp.maximum(top, jnp.max(scores, axis=1, keepdims=True))
        expo = jnp.exp2(scores - jnp.tile(new_top, (1, -(-count // 128)))[:, :count])
        fade = jnp.exp2(top - new_top)
        if count % 128 == 0:
            part = expo[:, :128]
            for lane in range(128, count, 128):
                part = part + expo[:, lane : lane + 128]
        else:
            part = jnp.sum(expo, axis=1, keepdims=True) * (1.0 / 128.0)
        mx[rows] = new_top
        den[rows] = den[rows] * fade + part
        acc[rows] = acc[rows] * jnp.tile(fade, (1, C // 128)) + dot(expo.astype(BF16), keys)

    def table():
        def summed(parts):
            return parts[0] if len(parts) == 1 else parts[0] + parts[1]

        spans = {(0, 0): (0,), (0, 1): (1, 2), (1, 0): (0, 1), (1, 1): (2,)}
        for a in range(2):
            for e in range(2):
                rows = [summed([up[dy, dx].astype(F32) for dy in spans[a, e]]) for dx in range(3)]
                for k, (b, f) in enumerate(((0, 1), (1, 0), (0, 0), (1, 1))):
                    cell = summed([rows[dx] for dx in spans[b, f]]).astype(BF16)
                    wu[a, k * C // 2 : (k + 1) * C // 2, e * C : (e + 1) * C] = cell

    for kind, c, *rest in ORDER:
        if kind == "query":
            q_copy = project()
        elif kind == "attend":
            attend(c, *rest)
        elif kind == "table":
            up_load.wait()
            table()
        else:
            step(kind, c, *rest)
            if (kind, c) == ("g+", 2) and rest == [0]:
                q_copy.wait_recv()
    attend(PARTS - 1, 3, 1, OWN, OWN)
    back = [
        send(acc.at[pl.ds(OWN, OWN)], acc_in, sib),
        send(mx.at[pl.ds(OWN, OWN)], mx_in, sib),
        send(den.at[pl.ds(OWN, OWN)], den_in, sib),
    ]
    attend(PARTS - 1, 3, 1, 0, OWN)
    proj_load.wait()
    for copy in back:
        copy.wait_recv()
    top = jnp.maximum(mx[:OWN], mx_in[...])
    mine = jnp.exp2(mx[:OWN] - top)
    other = jnp.exp2(mx_in[...] - top)
    total = jnp.sum(den[:OWN] * mine + den_in[...] * other, axis=1, keepdims=True)
    mine = jnp.tile(mine / total, (1, C // 128))
    other = jnp.tile(other / total, (1, C // 128))
    pooled = (acc[:OWN] * mine + acc_in[...] * other).astype(BF16)
    attn = dot(pooled, qkv[:, 2 * C :]).astype(BF16)
    value = (flat(lat[...]).astype(F32) + dot(attn, proj[...])).astype(BF16)
    mid[...] = value.reshape(2, COLS, C)
    act[1, 1:3] = silu(rms(value, conv_gain[...].reshape(1, C))).astype(BF16).reshape(2, COLS, C)


    far_own, near_own = 1 + core, 2 - core
    far_halo, near_halo = 3 * core, 3 - 3 * core
    edge = lax.rem(s, 31) == 0

    def to_far(buffer):
        return send(buffer.at[far_own], buffer.at[near_halo], far)

    def to_near(buffer):
        return send(buffer.at[near_own], buffer.at[far_halo], sib)

    def beside(own):
        return (
            send(act.at[1, own], act.at[0, own], z_plus),
            send(mid.at[own - 1], mid_in.at[own - 1], z_minus),
        )

    def arrived(pair, own, forward):
        pair[0].wait_recv()
        older = forward(act.at[0])
        pair[1].wait_recv()
        act[2, own] = silu(rms(mid_in[own - 1], conv_gain[...].reshape(1, C))).astype(BF16)
        return older, forward(act.at[2])

    def close(f):
        @pl.when(edge)
        def _():
            act[f, far_halo] = jnp.zeros((COLS, C), BF16)

    def taps(f, own):
        return jnp.concatenate([act[f, own - 1 + dy] for dy in range(3)], axis=1)

    def convolve(own):
        older = taps(0, own)
        older = jnp.where((z != 1) & (z != 2), older, jnp.zeros_like(older))
        both = jnp.concatenate([older, taps(2, own)], axis=1)
        value = conv[own - 1] + dot(both, wc[0:2].reshape(6 * C, 3 * C))
        value = value[:, C : 2 * C] + moved(value[:, :C], 1) + moved(value[:, 2 * C :], -1)
        value = value + conv_bias[...].reshape(1, C) + mid_in[own - 1].astype(F32)
        blocks[1, own - 1] = value.astype(BF16)

    def spread(own):
        return (
            send(blocks.at[1, own - 1], blocks.at[0, own - 1], z_plus),
            send(blocks.at[1, own - 1], blocks.at[2, own - 1], z_minus),
        )

    def double(pair, own):
        for copy in pair:
            copy.wait_recv()
        older = blocks[0, own - 1]
        older = jnp.where(z >= 2, older, jnp.zeros_like(older))
        both = jnp.concatenate([older, blocks[2, own - 1]], axis=1)
        value = (conv[own - 1, :, : 2 * C] + dot(both, wt[0:2].reshape(2 * C, 2 * C))).astype(BF16)
        frames[own, 0] = value[:, :C]
        frames[own, 1] = value[:, C:]

    bias = up_bias[...].reshape(1, C // 2)

    def upsample(i, a):
        rows = jnp.concatenate([flat(frames[i + a]), flat(frames[i + a + 1])], axis=1)
        value = lax.dot_general(rows, wu[a], NT, preferred_element_type=F32)
        side = value[:, C:]
        lane = lax.broadcasted_iota(jnp.int32, side.shape, 1)
        value = value[:, :C] + jnp.where(lane < C // 2, moved(side, 1), moved(side, -1))
        second = pltpu.roll(value, C // 2, 1)
        for frame in range(2):
            run = slice(frame * COLS, (frame + 1) * COLS)
            for part in range(2):
                lanes = slice(128 * part, 128 * part + 128)
                wide[part, pl.ds(0, COLS, stride=2), :] = value[run, lanes]
                wide[part, pl.ds(1, COLS, stride=2), :] = second[run, lanes]
            out[frame, 2 * i + a, :, :128] = (wide[0] + bias[:, :128]).astype(BF16)
            out[frame, 2 * i + a, :, 128:] = (wide[1, :, : C // 2 - 128] + bias[:, 128:]).astype(BF16)

    far_pair = beside(far_own)
    own_edges = to_far(act.at[1]), to_near(act.at[1])
    near_pair = beside(near_own)
    for row in conv_loads:
        for copy in row:
            copy.wait()
    for copy in own_edges:
        copy.wait_recv()
    close(1)

    @pl.when(z != 1)
    def _():
        rows = jnp.concatenate([flat(act[1, dy : dy + 2]) for dy in range(3)], axis=1)
        conv[...] = dot(rows, wc[2].reshape(3 * C, 3 * C)).reshape(conv.shape)

    @pl.when(z == 1)
    def _():
        conv[...] = jnp.zeros(conv.shape, F32)

    far_edges = arrived(far_pair, far_own, to_far)
    near_edges = arrived(near_pair, near_own, to_near)
    for copy in near_edges:
        copy.wait_recv()
    convolve(near_own)
    for copy in far_edges:
        copy.wait_recv()
    close(0)
    close(2)
    convolve(far_own)
    far_pair = spread(far_own)
    near_pair = spread(near_own)
    for copy in time_loads:
        copy.wait()
    rows = flat(blocks[1])
    rows = jnp.where(z >= 1, rows, jnp.zeros_like(rows))
    conv[:, :, : 2 * C] = (dot(rows, wt[2]) + time_bias[...].reshape(1, 2 * C)).reshape(2, COLS, 2 * C)
    double(far_pair, far_own)
    far_edge = to_far(frames)
    double(near_pair, near_own)
    near_edge = to_near(frames)
    upsample(0, 1)
    upsample(1, 0)
    near_edge.wait_recv()
    upsample(1 - core, 1 - core)
    far_edge.wait_recv()

    @pl.when(edge)
    def _():
        frames[far_halo] = jnp.zeros((2, COLS, C), BF16)

    upsample(core, core)
    for copy in pending:
        copy.wait_send()


SENDS = 96
LOADS = 16


def body(
    latent, attn_gain, qkv_weight, proj_weight, conv_gain, conv_weight, conv_bias, time_weight, time_bias, up_weight,
    up_bias,
):
    vmem = pl.BlockSpec(memory_space=pltpu.VMEM)
    anywhere = pl.BlockSpec(memory_space=pl.ANY)
    return pl.pallas_call(
        kernel,
        out_shape=jax.ShapeDtypeStruct((2, 4, 2 * COLS, C // 2), BF16),
        in_specs=[
            anywhere, vmem, anywhere, anywhere, vmem, anywhere, vmem, anywhere, vmem, anywhere, vmem,
        ],
        out_specs=vmem,
        scratch_shapes=[
            pltpu.VMEM((PARTS, PART, C), BF16),
            pltpu.VMEM((4 * PARTS, 4, PART, C), BF16),
            pltpu.VMEM((2 * OWN, C), BF16),
            pltpu.VMEM((2 * OWN, C), F32),
            pltpu.VMEM((2 * OWN, 128), F32),
            pltpu.VMEM((2 * OWN, 128), F32),
            pltpu.VMEM((OWN, C), F32),
            pltpu.VMEM((OWN, 128), F32),
            pltpu.VMEM((OWN, 128), F32),
            pltpu.VMEM((C, 3 * C), BF16),
            pltpu.VMEM((C, C), BF16),
            pltpu.VMEM((3, 3, C, 3 * C), BF16),
            pltpu.VMEM((3, C, 2 * C), BF16),
            pltpu.VMEM((3, 3, C // 2, C), BF16),
            pltpu.VMEM((2, 2 * C, 2 * C), BF16),
            pltpu.VMEM((2, COLS, C), BF16),
            pltpu.VMEM((2, COLS, C), BF16),
            pltpu.VMEM((3, 4, COLS, C), BF16),
            pltpu.VMEM((2, COLS, 3 * C), F32),
            pltpu.VMEM((3, 2, COLS, C), BF16),
            pltpu.VMEM((4, 2, COLS, C), BF16),
            pltpu.VMEM((2, 2 * COLS, 128), F32),
            pltpu.SemaphoreType.DMA((SENDS,)),
            pltpu.SemaphoreType.DMA((SENDS,)),
            pltpu.SemaphoreType.DMA((LOADS,)),
        ],
        compiler_params=pltpu.CompilerParams(
            collective_id=0, has_side_effects=True, vmem_limit_bytes=56 * 1024 * 1024
        ),
    )(
        latent, attn_gain, qkv_weight, proj_weight, conv_gain, conv_weight, conv_bias, time_weight, time_bias,
        jnp.swapaxes(up_weight, 2, 3), up_bias,
    )


def solution(mesh):
    return jax.shard_map(
        body,
        mesh=mesh,
        in_specs=(P("tm", "space", None, None), P(), P(), P(), P(), P(), P(), P(), P(), P(), P()),
        out_specs=P("tm", "space", None, None),
        check_vma=False,
    )
```

```python
import math

import jax
import jax.numpy as jnp
from jax import lax
from jax.experimental import pallas as pl
from jax.experimental.pallas import tpu as pltpu
from jax.sharding import PartitionSpec as P

MESH = pl.DeviceIdType.MESH
F32 = jnp.float32
BF16 = jnp.bfloat16
C = 384
COLS = 160
NT = (((1,), (1,)), ((), ()))
PARTS = 4
PART = 80
OWN = PARTS * PART
HALF = 80
SIDES = (0, 3, 1, 2)
TIMES = (0, 2, 1)
ORDER = (
    ("own", 0), ("own", 1), ("f-", 0), ("f+", 0), ("own", 2), ("f-", 1), ("own", 3), ("f+", 1), ("op", 1),
    ("g+", 0, 1), ("g+", 1, 0), ("op", 0), ("query", 0), ("g-", 0, 3), ("f+", 2), ("attend", 0, 0, 1), ("g+", 0, 3),
    ("g-", 0, 0), ("g-", 2, 0), ("g+", 0, 0), ("g-", 1, 3), ("g+", 3, 0), ("g-", 1, 0), ("g+", 1, 1), ("g+", 1, 3),
    ("g-", 1, 1), ("g-", 1, 2), ("g+", 1, 2), ("f-", 3), ("attend", 1, 1, 2), ("table", 0), ("g-", 0, 2),
    ("go", 0, 3), ("g+", 0, 2), ("g-", 0, 1), ("op", 2), ("attend", 0, 1, 2), ("f+", 3), ("g+", 2, 3), ("go", 0, 0),
    ("f-", 2), ("go", 1, 0), ("g-", 2, 3), ("g+", 2, 0), ("go", 1, 1), ("go", 1, 3), ("go", 1, 2),
    ("attend", 1, 3, 2), ("op", 3), ("g+", 3, 1), ("go", 0, 2), ("g-", 3, 0), ("go", 0, 1), ("attend", 0, 3, 2),
    ("g+", 3, 3), ("g-", 3, 3), ("g-", 2, 2), ("g+", 2, 2), ("g-", 3, 1), ("g-", 2, 1), ("g+", 2, 1),
    ("attend", 2, 1, 2), ("go", 2, 3), ("g-", 3, 2), ("g+", 3, 2), ("go", 2, 0), ("go", 3, 0), ("attend", 3, 1, 2),
    ("go", 3, 3), ("go", 2, 1), ("go", 2, 2), ("attend", 2, 3, 2), ("go", 3, 2), ("go", 3, 1),
)


def rms(x, gain):
    values = x.astype(F32)
    return values * lax.rsqrt(jnp.mean(values * values, axis=-1, keepdims=True) + 1e-06) * gain


def silu(x):
    return x / (1.0 + jnp.exp(-x))


def dot(a, b):
    return jnp.dot(a, b, preferred_element_type=F32)


def flat(x):
    return x.reshape(-1, x.shape[-1])


def moved(x, steps):
    index = lax.broadcasted_iota(jnp.int32, x.shape, 0)
    edge = 0 if steps == 1 else COLS - 1
    rolled = pltpu.roll(x, steps % x.shape[0], 0)
    keep = index != edge
    for run in range(1, x.shape[0] // COLS):
        keep = keep & (index != edge + run * COLS)
    return jnp.where(keep, rolled, 0.0)


def kernel(
    latent, attn_gain_hbm, qkv_hbm, proj_hbm, conv_gain_hbm, conv_hbm, conv_bias_hbm, time_hbm, time_bias_hbm, up_hbm,
    up_bias_hbm, out_hbm,
    attn_gain, conv_gain, conv_bias, time_bias, up_bias, out,
    lat, nb, qb, acc, mx, den, acc_out, stat_out, acc_in, stat_in,
    qkv, proj, wc, wt, up, wu,
    mid, mid_in, act, conv, blocks, frames, wide,
    ss, rs, ws,
):
    z = lax.axis_index("tm")
    s = lax.axis_index("space")
    core = lax.rem(s, 2)
    x = lax.rem(s // 2, 4)
    y = s // 8
    pos1 = x + core * (y - x)
    pos2 = y + core * (x - y)
    step1 = 2 + 6 * core
    step2 = 8 - 6 * core

    def at(zz, ss_):
        return (zz, ss_)

    sib = at(z, s + 1 - 2 * core)
    far = at(z, lax.rem(s + 2 * core + 31, 32))
    f_plus = at(z, s + (lax.rem(pos1 + 1, 4) - pos1) * step1)
    f_minus = at(z, s + (lax.rem(pos1 + 3, 4) - pos1) * step1)
    g_plus = at(z, s + (lax.rem(pos2 + 1, 4) - pos2) * step2)
    g_minus = at(z, s + (lax.rem(pos2 + 3, 4) - pos2) * step2)
    z_plus = at(lax.rem(z + 1, 8), s)
    z_minus = at(lax.rem(z + 7, 8), s)
    z_plus2 = at(lax.rem(z + 2, 8), s)
    z_minus2 = at(lax.rem(z + 6, 8), s)

    pending = []
    local = []

    def send(src, dst, device):
        k = len(pending)
        copy = pltpu.make_async_remote_copy(
            src_ref=src, dst_ref=dst, send_sem=ss.at[k], recv_sem=rs.at[k], device_id=device, device_id_type=MESH
        )
        copy.start()
        pending.append(copy)
        return copy


    def load(src, dst):
        copy = pltpu.make_async_copy(src, dst, ws.at[len(local)])
        copy.start()
        local.append(copy)
        return copy

    barrier = pltpu.get_barrier_semaphore()
    partners = (sib, far, f_plus, f_minus, g_plus, g_minus, z_plus, z_minus, z_plus2, z_minus2)
    for partner in partners:
        pl.semaphore_signal(barrier, inc=1, device_id=partner, device_id_type=MESH)
    gain_load = load(attn_gain_hbm, attn_gain)
    qkv_load = load(qkv_hbm, qkv)
    pl.semaphore_wait(barrier, len(partners))

    shift = [
        send(latent.at[0, c // 2, pl.ds(c % 2 * PART, PART)], lat.at[c], z_plus2) for c in range(PARTS)
    ]
    proj_load = load(proj_hbm, proj)
    conv_loads = [
        [load(conv_hbm.at[dt, :, dx], wc.at[TIMES.index(dt), :, :, pl.ds(dx * C, C)]) for dx in range(3)]
        for dt in TIMES
    ]
    time_loads = [load(time_hbm.at[dt], wt.at[TIMES.index(dt)]) for dt in TIMES]
    up_load = load(up_hbm, up)
    small_loads = [
        load(conv_gain_hbm, conv_gain),
        load(conv_bias_hbm, conv_bias),
        load(time_bias_hbm, time_bias),
        load(up_bias_hbm, up_bias),
    ]

    mx[...] = jnp.full(mx.shape, -1e30, F32)
    den[...] = jnp.zeros(den.shape, F32)
    acc[...] = jnp.zeros(acc.shape, F32)

    copies = {}

    def slot(c, j, i):
        return nb.at[4 * c + SIDES.index(j), i]

    def along_second(c, i):
        copies["g+", c, i] = send(slot(c, 0, i), slot(c, 3, i), g_plus)
        copies["g-", c, i] = send(slot(c, 0, i), slot(c, 1, i), g_minus)

    def step(kind, c, i=0):
        if kind == "own":
            shift[c].wait_recv()
            nb[4 * c, 0] = rms(lat[c], attn_gain[...].reshape(1, C)).astype(BF16)
            copies["f+", c, 0] = send(slot(c, 0, 0), slot(c, 0, 3), f_plus)
            copies["f-", c, 0] = send(slot(c, 0, 0), slot(c, 0, 1), f_minus)
            along_second(c, 0)
            return
        copies[kind, c, i].wait_recv()
        if kind == "f+":
            if c % 2 == 0:
                copies["op", c, 0] = send(slot(c, 0, 3), slot(c, 0, 2), f_plus)
            along_second(c, 3)
        elif kind == "f-":
            if c % 2 == 1:
                copies["op", c, 0] = send(slot(c, 0, 1), slot(c, 0, 2), f_minus)
            along_second(c, 1)
        elif kind == "op":
            along_second(c, 2)
        elif kind == "g+" and (c + i) % 2 == 0:
            copies["go", c, i] = send(slot(c, 3, i), slot(c, 2, i), g_plus)
        elif kind == "g-" and (c + i) % 2 == 1:
            copies["go", c, i] = send(slot(c, 1, i), slot(c, 2, i), g_minus)

    def project():
        qkv_load.wait()
        scale = math.log2(math.e) / math.sqrt(C)
        normed = jnp.concatenate([nb[4 * c, 0] for c in range(PARTS)], axis=0)
        query = dot(normed, qkv[:, :C]).astype(BF16)
        query = lax.dot_general(query, qkv[:, C : 2 * C], NT, preferred_element_type=F32) * scale
        qb[:OWN] = query.astype(BF16)
        return send(qb.at[pl.ds(0, OWN)], qb.at[pl.ds(OWN, OWN)], sib)

    def attend(c, p, n, low=0, size=2 * OWN):
        rows = slice(low, low + size)
        count = n * OWN
        keys = nb[4 * c + p : 4 * c + p + n].reshape(count, C)
        scores = lax.dot_general(qb[rows], keys, NT, preferred_element_type=F32)
        top = mx[rows]
        new_top = jnp.maximum(top, jnp.max(scores, axis=1, keepdims=True))
        expo = jnp.exp2(scores - jnp.tile(new_top, (1, -(-count // 128)))[:, :count])
        fade = jnp.exp2(top - new_top)
        if count % 128 == 0:
            part = expo[:, :128]
            for lane in range(128, count, 128):
                part = part + expo[:, lane : lane + 128]
        else:
            part = jnp.sum(expo, axis=1, keepdims=True) * (1.0 / 128.0)
        mx[rows] = new_top
        den[rows] = den[rows] * fade + part
        acc[rows] = acc[rows] * jnp.tile(fade, (1, C // 128)) + dot(expo.astype(BF16), keys)

    def table():
        def summed(parts):
            return parts[0] if len(parts) == 1 else parts[0] + parts[1]

        spans = {(0, 0): (0,), (0, 1): (1, 2), (1, 0): (0, 1), (1, 1): (2,)}
        for a in range(2):
            for e in range(2):
                rows = [summed([up[dy, dx].astype(F32) for dy in spans[a, e]]) for dx in range(3)]
                for k, (b, f) in enumerate(((0, 1), (1, 0), (0, 0), (1, 1))):
                    cell = summed([rows[dx] for dx in spans[b, f]]).astype(BF16)
                    wu[a, k * C // 2 : (k + 1) * C // 2, e * C : (e + 1) * C] = cell

    gain_load.wait()
    for kind, c, *rest in ORDER:
        if kind == "query":
            q_copy = project()
        elif kind == "attend":
            if q_copy is not None:
                q_copy = q_copy.wait_recv()
            attend(c, *rest)
        elif kind == "table":
            up_load.wait()
            table()
        else:
            step(kind, c, *rest)
    attend(PARTS - 1, 3, 1, OWN, OWN)
    acc_out[...] = acc[OWN:].astype(BF16)
    lane = lax.broadcasted_iota(jnp.int32, (OWN, 128), 1)
    stat_out[...] = jnp.where(lane < 64, mx[OWN:], jnp.sum(den[OWN:], axis=1, keepdims=True))
    back = [send(acc_out, acc_in, sib), send(stat_out, stat_in, sib)]
    attend(PARTS - 1, 3, 1, 0, OWN)
    for copy in [proj_load] + small_loads:
        copy.wait()
    for copy in back:
        copy.wait_recv()
    top = jnp.maximum(mx[:OWN, :1], stat_in[:, :1])
    mine = jnp.exp2(mx[:OWN, :1] - top)
    other = jnp.exp2(stat_in[:, :1] - top)
    total = jnp.sum(den[:OWN], axis=1, keepdims=True) * mine + stat_in[:, 64:65] * other
    pooled = (acc[:OWN] * (mine / total) + acc_in[...].astype(F32) * (other / total)).astype(BF16)
    attn = dot(pooled, qkv[:, 2 * C :]).astype(BF16)
    value = (flat(lat[...]).astype(F32) + dot(attn, proj[...])).astype(BF16)
    mid[...] = value.reshape(2, COLS, C)
    act[1, 1:3] = silu(rms(value, conv_gain[...].reshape(1, C))).astype(BF16).reshape(2, COLS, C)


    far_own, near_own = 1 + core, 2 - core
    far_halo, near_halo = 3 * core, 3 - 3 * core
    edge = lax.rem(s, 31) == 0

    def to_far(buffer):
        return send(buffer.at[far_own], buffer.at[near_halo], far)

    def to_near(buffer):
        return send(buffer.at[near_own], buffer.at[far_halo], sib)

    def halves():
        return [pl.ds(0, HALF), pl.ds(HALF, HALF)]

    def beside(own, run):
        return (
            send(act.at[1, own, run], act.at[0, own, run], z_plus),
            send(mid.at[own - 1, run], mid_in.at[own - 1, run], z_minus),
        )

    def arrived(pair, own, run, halo, device):
        pair[0].wait_recv()
        older = send(act.at[0, own, run], act.at[0, halo, run], device)
        pair[1].wait_recv()
        act[2, own, run] = silu(rms(mid_in[own - 1, run], conv_gain[...].reshape(1, C))).astype(BF16)
        return older, send(act.at[2, own, run], act.at[2, halo, run], device)

    def close(f):
        @pl.when(edge)
        def _():
            act[f, far_halo] = jnp.zeros((COLS, C), BF16)

    def taps(f, own):
        return jnp.concatenate([act[f, own - 1 + dy] for dy in range(3)], axis=1)

    def convolve(own):
        older = taps(0, own)
        older = jnp.where((z != 1) & (z != 2), older, jnp.zeros_like(older))
        both = jnp.concatenate([older, taps(2, own)], axis=1)
        value = conv[own - 1] + dot(both, wc[0:2].reshape(6 * C, 3 * C))
        value = value[:, C : 2 * C] + moved(value[:, :C], 1) + moved(value[:, 2 * C :], -1)
        value = value + conv_bias[...].reshape(1, C) + mid_in[own - 1].astype(F32)
        blocks[1, own - 1] = value.astype(BF16)

    def spread(own, run):
        return (
            send(blocks.at[1, own - 1, run], blocks.at[0, own - 1, run], z_plus),
            send(blocks.at[1, own - 1, run], blocks.at[2, own - 1, run], z_minus),
        )

    def double(pair, own, run, halo, device):
        for copy in pair:
            copy.wait_recv()
        older = blocks[0, own - 1, run]
        older = jnp.where(z >= 2, older, jnp.zeros_like(older))
        both = jnp.concatenate([older, blocks[2, own - 1, run]], axis=1)
        value = (conv[own - 1, run, : 2 * C] + dot(both, wt[0:2].reshape(2 * C, 2 * C))).astype(BF16)
        frames[own, 0, run] = value[:, :C]
        frames[own, 1, run] = value[:, C:]
        return send(frames.at[own, :, run], frames.at[halo, :, run], device)

    bias = up_bias[...].reshape(1, C // 2)

    stores = []

    def upsample(i, a):
        rows = jnp.concatenate([flat(frames[i + a]), flat(frames[i + a + 1])], axis=1)
        value = lax.dot_general(rows, wu[a], NT, preferred_element_type=F32)
        side = value[:, C:]
        lane = lax.broadcasted_iota(jnp.int32, side.shape, 1)
        value = value[:, :C] + jnp.where(lane < C // 2, moved(side, 1), moved(side, -1))
        second = pltpu.roll(value, C // 2, 1)
        for frame in range(2):
            run = slice(frame * COLS, (frame + 1) * COLS)
            for part in range(2):
                lanes = slice(128 * part, 128 * part + 128)
                wide[part, pl.ds(0, COLS, stride=2), :] = value[run, lanes]
                wide[part, pl.ds(1, COLS, stride=2), :] = second[run, lanes]
            out[frame, 2 * i + a, :, :128] = (wide[0] + bias[:, :128]).astype(BF16)
            out[frame, 2 * i + a, :, 128:] = (wide[1, :, : C // 2 - 128] + bias[:, 128:]).astype(BF16)
        stores.append(load(out.at[:, 2 * i + a], out_hbm.at[:, 2 * i + a]))

    whole = pl.ds(0, COLS)
    far_pairs = [beside(far_own, run) for run in halves()]
    own_edges = to_far(act.at[1]), to_near(act.at[1])
    near_pair = beside(near_own, whole)
    for row in conv_loads:
        for copy in row:
            copy.wait()
    for copy in own_edges:
        copy.wait_recv()
    close(1)

    @pl.when(z != 1)
    def _():
        rows = jnp.concatenate([flat(act[1, dy : dy + 2]) for dy in range(3)], axis=1)
        conv[...] = dot(rows, wc[2].reshape(3 * C, 3 * C)).reshape(conv.shape)

    @pl.when(z == 1)
    def _():
        conv[...] = jnp.zeros(conv.shape, F32)

    far_edges = []
    for pair, run in zip(far_pairs, halves()):
        far_edges += arrived(pair, far_own, run, near_halo, far)
    near_edges = arrived(near_pair, near_own, whole, far_halo, sib)
    for copy in near_edges:
        copy.wait_recv()
    convolve(near_own)
    for copy in far_edges:
        copy.wait_recv()
    close(0)
    close(2)
    convolve(far_own)
    far_pairs = [spread(far_own, run) for run in halves()]
    near_pair = spread(near_own, whole)
    for copy in time_loads:
        copy.wait()
    rows = flat(blocks[1])
    rows = jnp.where(z >= 1, rows, jnp.zeros_like(rows))
    conv[:, :, : 2 * C] = (dot(rows, wt[2]) + time_bias[...].reshape(1, 2 * C)).reshape(2, COLS, 2 * C)
    far_edges = [double(pair, far_own, run, near_halo, far) for pair, run in zip(far_pairs, halves())]
    near_edge = double(near_pair, near_own, whole, far_halo, sib)
    upsample(0, 1)
    upsample(1, 0)
    near_edge.wait_recv()
    upsample(1 - core, 1 - core)
    for copy in far_edges:
        copy.wait_recv()

    @pl.when(edge)
    def _():
        frames[far_halo] = jnp.zeros((2, COLS, C), BF16)

    upsample(core, core)
    for copy in pending:
        copy.wait_send()
    for copy in stores:
        copy.wait()


SENDS = 96
LOADS = 32


def body(
    latent, attn_gain, qkv_weight, proj_weight, conv_gain, conv_weight, conv_bias, time_weight, time_bias, up_weight,
    up_bias,
):
    anywhere = pl.BlockSpec(memory_space=pl.ANY)
    return pl.pallas_call(
        kernel,
        out_shape=jax.ShapeDtypeStruct((2, 4, 2 * COLS, C // 2), BF16),
        in_specs=[anywhere] * 11,
        out_specs=anywhere,
        scratch_shapes=[
            pltpu.VMEM((C,), F32),
            pltpu.VMEM((C,), F32),
            pltpu.VMEM((C,), F32),
            pltpu.VMEM((2 * C,), F32),
            pltpu.VMEM((C // 2,), F32),
            pltpu.VMEM((2, 4, 2 * COLS, C // 2), BF16),
            pltpu.VMEM((PARTS, PART, C), BF16),
            pltpu.VMEM((4 * PARTS, 4, PART, C), BF16),
            pltpu.VMEM((2 * OWN, C), BF16),
            pltpu.VMEM((2 * OWN, C), F32),
            pltpu.VMEM((2 * OWN, 128), F32),
            pltpu.VMEM((2 * OWN, 128), F32),
            pltpu.VMEM((OWN, C), BF16),
            pltpu.VMEM((OWN, 128), F32),
            pltpu.VMEM((OWN, C), BF16),
            pltpu.VMEM((OWN, 128), F32),
            pltpu.VMEM((C, 3 * C), BF16),
            pltpu.VMEM((C, C), BF16),
            pltpu.VMEM((3, 3, C, 3 * C), BF16),
            pltpu.VMEM((3, C, 2 * C), BF16),
            pltpu.VMEM((3, 3, C // 2, C), BF16),
            pltpu.VMEM((2, 2 * C, 2 * C), BF16),
            pltpu.VMEM((2, COLS, C), BF16),
            pltpu.VMEM((2, COLS, C), BF16),
            pltpu.VMEM((3, 4, COLS, C), BF16),
            pltpu.VMEM((2, COLS, 3 * C), F32),
            pltpu.VMEM((3, 2, COLS, C), BF16),
            pltpu.VMEM((4, 2, COLS, C), BF16),
            pltpu.VMEM((2, 2 * COLS, 128), F32),
            pltpu.SemaphoreType.DMA((SENDS,)),
            pltpu.SemaphoreType.DMA((SENDS,)),
            pltpu.SemaphoreType.DMA((LOADS,)),
        ],
        compiler_params=pltpu.CompilerParams(
            collective_id=0, has_side_effects=True, vmem_limit_bytes=56 * 1024 * 1024
        ),
    )(
        latent, attn_gain, qkv_weight, proj_weight, conv_gain, conv_weight, conv_bias, time_weight, time_bias,
        jnp.swapaxes(up_weight, 2, 3), up_bias,
    )


def solution(mesh):
    return jax.shard_map(
        body,
        mesh=mesh,
        in_specs=(P("tm", "space", None, None), P(), P(), P(), P(), P(), P(), P(), P(), P(), P()),
        out_specs=P("tm", "space", None, None),
        check_vma=False,
    )
```

```python
import math

import jax
import jax.numpy as jnp
from jax import lax
from jax.experimental import pallas as pl
from jax.experimental.pallas import tpu as pltpu
from jax.sharding import PartitionSpec as P

MESH = pl.DeviceIdType.MESH
F32 = jnp.float32
BF16 = jnp.bfloat16
C = 384
COLS = 160
NT = (((1,), (1,)), ((), ()))
PARTS = 4
PART = 80
OWN = PARTS * PART
HALF = 80
SIDES = (0, 3, 1, 2)
TIMES = (0, 2, 1)
ORDER = (
    ("own", 0), ("own", 1), ("f-", 0), ("f+", 0), ("own", 2), ("f-", 1), ("own", 3), ("f+", 1), ("op", 1),
    ("g+", 0, 1), ("g+", 1, 0), ("op", 0), ("query", 0), ("g-", 0, 3), ("f+", 2), ("attend", 0, 0, 1), ("g+", 0, 3),
    ("g-", 0, 0), ("g-", 2, 0), ("g+", 0, 0), ("g-", 1, 3), ("g+", 3, 0), ("g-", 1, 0), ("g+", 1, 1), ("g+", 1, 3),
    ("g-", 1, 1), ("g-", 1, 2), ("g+", 1, 2), ("f-", 3), ("attend", 1, 1, 2), ("table", 0), ("g-", 0, 2),
    ("go", 0, 3), ("g+", 0, 2), ("g-", 0, 1), ("op", 2), ("attend", 0, 1, 2), ("f+", 3), ("g+", 2, 3), ("go", 0, 0),
    ("f-", 2), ("go", 1, 0), ("g-", 2, 3), ("g+", 2, 0), ("go", 1, 1), ("go", 1, 3), ("go", 1, 2),
    ("attend", 1, 3, 2), ("op", 3), ("g+", 3, 1), ("go", 0, 2), ("g-", 3, 0), ("go", 0, 1), ("attend", 0, 3, 2),
    ("g+", 3, 3), ("g-", 3, 3), ("g-", 2, 2), ("g+", 2, 2), ("g-", 3, 1), ("g-", 2, 1), ("g+", 2, 1),
    ("attend", 2, 1, 2), ("go", 2, 3), ("g-", 3, 2), ("g+", 3, 2), ("go", 2, 0), ("go", 3, 0), ("attend", 3, 1, 2),
    ("go", 3, 3), ("go", 2, 1), ("go", 2, 2), ("attend", 2, 3, 2), ("go", 3, 2), ("go", 3, 1),
)


def rms(x, gain):
    values = x.astype(F32)
    return values * lax.rsqrt(jnp.mean(values * values, axis=-1, keepdims=True) + 1e-06) * gain


def silu(x):
    return x / (1.0 + jnp.exp(-x))


def dot(a, b):
    return jnp.dot(a, b, preferred_element_type=F32)


def flat(x):
    return x.reshape(-1, x.shape[-1])


def moved(x, steps):
    index = lax.broadcasted_iota(jnp.int32, x.shape, 0)
    edge = 0 if steps == 1 else COLS - 1
    rolled = pltpu.roll(x, steps % x.shape[0], 0)
    keep = index != edge
    for run in range(1, x.shape[0] // COLS):
        keep = keep & (index != edge + run * COLS)
    return jnp.where(keep, rolled, 0.0)


def kernel(
    latent, attn_gain_hbm, qkv_hbm, proj_hbm, conv_gain_hbm, conv_hbm, conv_bias_hbm, time_hbm, time_bias_hbm, up_hbm,
    up_bias_hbm, out_hbm,
    attn_gain, conv_gain, conv_bias, time_bias, up_bias, out,
    lat, nb, qb, acc, mx, den, acc_out, stat_out, acc_in, stat_in,
    qkv, proj, wc, wt, up, wu,
    mid, mid_in, act, conv, blocks, frames, wide,
    ss, rs, ws,
):
    z = lax.axis_index("tm")
    s = lax.axis_index("space")
    core = lax.rem(s, 2)
    x = lax.rem(s // 2, 4)
    y = s // 8
    pos1 = x + core * (y - x)
    pos2 = y + core * (x - y)
    step1 = 2 + 6 * core
    step2 = 8 - 6 * core

    def at(zz, ss_):
        return (zz, ss_)

    sib = at(z, s + 1 - 2 * core)
    far = at(z, lax.rem(s + 2 * core + 31, 32))
    f_plus = at(z, s + (lax.rem(pos1 + 1, 4) - pos1) * step1)
    f_minus = at(z, s + (lax.rem(pos1 + 3, 4) - pos1) * step1)
    g_plus = at(z, s + (lax.rem(pos2 + 1, 4) - pos2) * step2)
    g_minus = at(z, s + (lax.rem(pos2 + 3, 4) - pos2) * step2)
    z_plus = at(lax.rem(z + 1, 8), s)
    z_minus = at(lax.rem(z + 7, 8), s)
    z_plus2 = at(lax.rem(z + 2, 8), s)
    z_minus2 = at(lax.rem(z + 6, 8), s)

    pending = []
    local = []

    def send(src, dst, device):
        k = len(pending)
        copy = pltpu.make_async_remote_copy(
            src_ref=src, dst_ref=dst, send_sem=ss.at[k], recv_sem=rs.at[k], device_id=device, device_id_type=MESH
        )
        copy.start()
        pending.append(copy)
        return copy

    left = []

    def sent(*copies):
        for copy in copies:
            copy.wait_send()
            left.append(id(copy))


    def load(src, dst):
        copy = pltpu.make_async_copy(src, dst, ws.at[len(local)])
        copy.start()
        local.append(copy)
        return copy

    barrier = pltpu.get_barrier_semaphore()
    partners = (sib, far, f_plus, f_minus, g_plus, g_minus, z_plus, z_minus, z_plus2, z_minus2)
    for partner in partners:
        pl.semaphore_signal(barrier, inc=1, device_id=partner, device_id_type=MESH)
    gain_load = load(attn_gain_hbm, attn_gain)
    qkv_load = load(qkv_hbm, qkv)
    pl.semaphore_wait(barrier, len(partners))

    shift = []

    def shift_next():
        c = len(shift)
        if c < PARTS:
            if c:
                sent(shift[-1])
            shift.append(send(latent.at[0, c // 2, pl.ds(c % 2 * PART, PART)], lat.at[c], z_plus2))

    shift_next()
    proj_load = load(proj_hbm, proj)
    conv_loads = [
        [load(conv_hbm.at[dt, :, dx], wc.at[TIMES.index(dt), :, :, pl.ds(dx * C, C)]) for dx in range(3)]
        for dt in TIMES
    ]
    time_loads = [load(time_hbm.at[dt], wt.at[TIMES.index(dt)]) for dt in TIMES]
    up_load = load(up_hbm, up)
    small_loads = [
        load(conv_gain_hbm, conv_gain),
        load(conv_bias_hbm, conv_bias),
        load(time_bias_hbm, time_bias),
        load(up_bias_hbm, up_bias),
    ]

    mx[...] = jnp.full(mx.shape, -1e30, F32)
    den[...] = jnp.zeros(den.shape, F32)
    acc[...] = jnp.zeros(acc.shape, F32)

    copies = {}

    def slot(c, j, i):
        return nb.at[4 * c + SIDES.index(j), i]

    def along_second(c, i):
        copies["g+", c, i] = send(slot(c, 0, i), slot(c, 3, i), g_plus)
        copies["g-", c, i] = send(slot(c, 0, i), slot(c, 1, i), g_minus)

    def step(kind, c, i=0):
        if kind == "own":
            shift[c].wait_recv()
            nb[4 * c, 0] = rms(lat[c], attn_gain[...].reshape(1, C)).astype(BF16)
            copies["f+", c, 0] = send(slot(c, 0, 0), slot(c, 0, 3), f_plus)
            copies["f-", c, 0] = send(slot(c, 0, 0), slot(c, 0, 1), f_minus)
            along_second(c, 0)
            shift_next()
            return
        copies[kind, c, i].wait_recv()
        if kind == "f+":
            if c % 2 == 0:
                copies["op", c, 0] = send(slot(c, 0, 3), slot(c, 0, 2), f_plus)
            along_second(c, 3)
        elif kind == "f-":
            if c % 2 == 1:
                copies["op", c, 0] = send(slot(c, 0, 1), slot(c, 0, 2), f_minus)
            along_second(c, 1)
        elif kind == "op":
            along_second(c, 2)
        elif kind == "g+" and (c + i) % 2 == 0:
            copies["go", c, i] = send(slot(c, 3, i), slot(c, 2, i), g_plus)
        elif kind == "g-" and (c + i) % 2 == 1:
            copies["go", c, i] = send(slot(c, 1, i), slot(c, 2, i), g_minus)

    def project():
        qkv_load.wait()
        scale = math.log2(math.e) / math.sqrt(C)
        normed = jnp.concatenate([nb[4 * c, 0] for c in range(PARTS)], axis=0)
        query = dot(normed, qkv[:, :C]).astype(BF16)
        query = lax.dot_general(query, qkv[:, C : 2 * C], NT, preferred_element_type=F32) * scale
        qb[:OWN] = query.astype(BF16)
        return send(qb.at[pl.ds(0, OWN)], qb.at[pl.ds(OWN, OWN)], sib)

    def attend(c, p, n, low=0, size=2 * OWN):
        rows = slice(low, low + size)
        count = n * OWN
        keys = nb[4 * c + p : 4 * c + p + n].reshape(count, C)
        scores = lax.dot_general(qb[rows], keys, NT, preferred_element_type=F32)
        top = mx[rows]
        new_top = jnp.maximum(top, jnp.max(scores, axis=1, keepdims=True))
        expo = jnp.exp2(scores - jnp.tile(new_top, (1, -(-count // 128)))[:, :count])
        fade = jnp.exp2(top - new_top)
        if count % 128 == 0:
            part = expo[:, :128]
            for lane in range(128, count, 128):
                part = part + expo[:, lane : lane + 128]
        else:
            part = jnp.sum(expo, axis=1, keepdims=True) * (1.0 / 128.0)
        mx[rows] = new_top
        den[rows] = den[rows] * fade + part
        acc[rows] = acc[rows] * jnp.tile(fade, (1, C // 128)) + dot(expo.astype(BF16), keys)

    def table():
        def summed(parts):
            return parts[0] if len(parts) == 1 else parts[0] + parts[1]

        spans = {(0, 0): (0,), (0, 1): (1, 2), (1, 0): (0, 1), (1, 1): (2,)}
        for a in range(2):
            for e in range(2):
                rows = [summed([up[dy, dx].astype(F32) for dy in spans[a, e]]) for dx in range(3)]
                for k, (b, f) in enumerate(((0, 1), (1, 0), (0, 0), (1, 1))):
                    cell = summed([rows[dx] for dx in spans[b, f]]).astype(BF16)
                    wu[a, k * C // 2 : (k + 1) * C // 2, e * C : (e + 1) * C] = cell

    gain_load.wait()
    for _ in range(SHIFT_AHEAD):
        shift_next()
    for kind, c, *rest in ORDER:
        if kind == "query":
            q_copy = project()
        elif kind == "attend":
            if q_copy is not None:
                q_copy = q_copy.wait_recv()
            attend(c, *rest)
        elif kind == "table":
            up_load.wait()
            table()
        else:
            step(kind, c, *rest)
    attend(PARTS - 1, 3, 1, OWN, OWN)
    acc_out[...] = acc[OWN:].astype(BF16)
    lane = lax.broadcasted_iota(jnp.int32, (OWN, 128), 1)
    stat_out[...] = jnp.where(lane < 64, mx[OWN:], jnp.sum(den[OWN:], axis=1, keepdims=True))
    back = [send(acc_out, acc_in, sib), send(stat_out, stat_in, sib)]
    attend(PARTS - 1, 3, 1, 0, OWN)
    for copy in [proj_load] + small_loads:
        copy.wait()
    for copy in back:
        copy.wait_recv()
    top = jnp.maximum(mx[:OWN, :1], stat_in[:, :1])
    mine = jnp.exp2(mx[:OWN, :1] - top)
    other = jnp.exp2(stat_in[:, :1] - top)
    total = jnp.sum(den[:OWN], axis=1, keepdims=True) * mine + stat_in[:, 64:65] * other
    pooled = (acc[:OWN] * (mine / total) + acc_in[...].astype(F32) * (other / total)).astype(BF16)
    attn = dot(pooled, qkv[:, 2 * C :]).astype(BF16)
    value = (flat(lat[...]).astype(F32) + dot(attn, proj[...])).astype(BF16)
    mid[...] = value.reshape(2, COLS, C)
    act[1, 1:3] = silu(rms(value, conv_gain[...].reshape(1, C))).astype(BF16).reshape(2, COLS, C)


    far_own, near_own = 1 + core, 2 - core
    far_halo, near_halo = 3 * core, 3 - 3 * core
    edge = lax.rem(s, 31) == 0

    def to_far(buffer):
        return send(buffer.at[far_own], buffer.at[near_halo], far)

    def to_near(buffer):
        return send(buffer.at[near_own], buffer.at[far_halo], sib)

    def halves():
        return [pl.ds(0, HALF), pl.ds(HALF, HALF)]

    def beside(own, run):
        return (
            send(act.at[1, own, run], act.at[0, own, run], z_plus),
            send(mid.at[own - 1, run], mid_in.at[own - 1, run], z_minus),
        )

    def arrived(pair, own, run, halo, device):
        pair[0].wait_recv()
        older = send(act.at[0, own, run], act.at[0, halo, run], device)
        pair[1].wait_recv()
        act[2, own, run] = silu(rms(mid_in[own - 1, run], conv_gain[...].reshape(1, C))).astype(BF16)
        return older, send(act.at[2, own, run], act.at[2, halo, run], device)

    def close(f):
        @pl.when(edge)
        def _():
            act[f, far_halo] = jnp.zeros((COLS, C), BF16)

    def taps(f, own):
        return jnp.concatenate([act[f, own - 1 + dy] for dy in range(3)], axis=1)

    def convolve(own):
        older = taps(0, own)
        older = jnp.where((z != 1) & (z != 2), older, jnp.zeros_like(older))
        both = jnp.concatenate([older, taps(2, own)], axis=1)
        value = conv[own - 1] + dot(both, wc[0:2].reshape(6 * C, 3 * C))
        value = value[:, C : 2 * C] + moved(value[:, :C], 1) + moved(value[:, 2 * C :], -1)
        value = value + conv_bias[...].reshape(1, C) + mid_in[own - 1].astype(F32)
        blocks[1, own - 1] = value.astype(BF16)

    def spread(own, run):
        return (
            send(blocks.at[1, own - 1, run], blocks.at[0, own - 1, run], z_plus),
            send(blocks.at[1, own - 1, run], blocks.at[2, own - 1, run], z_minus),
        )

    def double(pair, own, run, halo, device):
        for copy in pair:
            copy.wait_recv()
        older = blocks[0, own - 1, run]
        older = jnp.where(z >= 2, older, jnp.zeros_like(older))
        both = jnp.concatenate([older, blocks[2, own - 1, run]], axis=1)
        value = (conv[own - 1, run, : 2 * C] + dot(both, wt[0:2].reshape(2 * C, 2 * C))).astype(BF16)
        frames[own, 0, run] = value[:, :C]
        frames[own, 1, run] = value[:, C:]
        return send(frames.at[own, :, run], frames.at[halo, :, run], device)

    bias = up_bias[...].reshape(1, C // 2)

    stores = []

    def upsample(i, a):
        rows = jnp.concatenate([flat(frames[i + a]), flat(frames[i + a + 1])], axis=1)
        value = lax.dot_general(rows, wu[a], NT, preferred_element_type=F32)
        side = value[:, C:]
        lane = lax.broadcasted_iota(jnp.int32, side.shape, 1)
        value = value[:, :C] + jnp.where(lane < C // 2, moved(side, 1), moved(side, -1))
        second = pltpu.roll(value, C // 2, 1)
        for frame in range(2):
            run = slice(frame * COLS, (frame + 1) * COLS)
            for part in range(2):
                lanes = slice(128 * part, 128 * part + 128)
                wide[part, pl.ds(0, COLS, stride=2), :] = value[run, lanes]
                wide[part, pl.ds(1, COLS, stride=2), :] = second[run, lanes]
            out[frame, 2 * i + a, :, :128] = (wide[0] + bias[:, :128]).astype(BF16)
            out[frame, 2 * i + a, :, 128:] = (wide[1, :, : C // 2 - 128] + bias[:, 128:]).astype(BF16)
        stores.append(load(out.at[:, 2 * i + a], out_hbm.at[:, 2 * i + a]))

    whole = pl.ds(0, COLS)
    far_pairs = [beside(far_own, run) for run in halves()]
    own_edges = to_far(act.at[1]), to_near(act.at[1])
    near_pair = beside(near_own, whole)
    for row in conv_loads:
        for copy in row:
            copy.wait()
    for copy in own_edges:
        copy.wait_recv()
    close(1)

    @pl.when(z != 1)
    def _():
        rows = jnp.concatenate([flat(act[1, dy : dy + 2]) for dy in range(3)], axis=1)
        conv[...] = dot(rows, wc[2].reshape(3 * C, 3 * C)).reshape(conv.shape)

    @pl.when(z == 1)
    def _():
        conv[...] = jnp.zeros(conv.shape, F32)

    far_edges = []
    for pair, run in zip(far_pairs, halves()):
        far_edges += arrived(pair, far_own, run, near_halo, far)
    near_edges = arrived(near_pair, near_own, whole, far_halo, sib)
    for copy in near_edges:
        copy.wait_recv()
    convolve(near_own)
    near_pair = spread(near_own, halves()[0])
    for copy in far_edges:
        copy.wait_recv()
    close(0)
    close(2)
    convolve(far_own)
    far_pairs = [spread(far_own, run) for run in halves()]
    for copy in time_loads:
        copy.wait()
    rows = flat(blocks[1])
    rows = jnp.where(z >= 1, rows, jnp.zeros_like(rows))
    near_pairs = [near_pair, spread(near_own, halves()[1])]
    conv[:, :, : 2 * C] = (dot(rows, wt[2]) + time_bias[...].reshape(1, 2 * C)).reshape(2, COLS, 2 * C)
    far_edges = [double(pair, far_own, run, near_halo, far) for pair, run in zip(far_pairs, halves())]
    near_edges = [double(pair, near_own, run, far_halo, sib) for pair, run in zip(near_pairs, halves())]
    upsample(0, 1)
    upsample(1, 0)
    for copy in near_edges:
        copy.wait_recv()
    upsample(1 - core, 1 - core)
    for copy in far_edges:
        copy.wait_recv()

    @pl.when(edge)
    def _():
        frames[far_halo] = jnp.zeros((2, COLS, C), BF16)

    upsample(core, core)
    for copy in pending:
        if id(copy) not in left:
            copy.wait_send()
    for copy in stores:
        copy.wait()


SHIFT_AHEAD = 2
SENDS = 96
LOADS = 32


def body(
    latent, attn_gain, qkv_weight, proj_weight, conv_gain, conv_weight, conv_bias, time_weight, time_bias, up_weight,
    up_bias,
):
    anywhere = pl.BlockSpec(memory_space=pl.ANY)
    return pl.pallas_call(
        kernel,
        out_shape=jax.ShapeDtypeStruct((2, 4, 2 * COLS, C // 2), BF16),
        in_specs=[anywhere] * 11,
        out_specs=anywhere,
        scratch_shapes=[
            pltpu.VMEM((C,), F32),
            pltpu.VMEM((C,), F32),
            pltpu.VMEM((C,), F32),
            pltpu.VMEM((2 * C,), F32),
            pltpu.VMEM((C // 2,), F32),
            pltpu.VMEM((2, 4, 2 * COLS, C // 2), BF16),
            pltpu.VMEM((PARTS, PART, C), BF16),
            pltpu.VMEM((4 * PARTS, 4, PART, C), BF16),
            pltpu.VMEM((2 * OWN, C), BF16),
            pltpu.VMEM((2 * OWN, C), F32),
            pltpu.VMEM((2 * OWN, 128), F32),
            pltpu.VMEM((2 * OWN, 128), F32),
            pltpu.VMEM((OWN, C), BF16),
            pltpu.VMEM((OWN, 128), F32),
            pltpu.VMEM((OWN, C), BF16),
            pltpu.VMEM((OWN, 128), F32),
            pltpu.VMEM((C, 3 * C), BF16),
            pltpu.VMEM((C, C), BF16),
            pltpu.VMEM((3, 3, C, 3 * C), BF16),
            pltpu.VMEM((3, C, 2 * C), BF16),
            pltpu.VMEM((3, 3, C // 2, C), BF16),
            pltpu.VMEM((2, 2 * C, 2 * C), BF16),
            pltpu.VMEM((2, COLS, C), BF16),
            pltpu.VMEM((2, COLS, C), BF16),
            pltpu.VMEM((3, 4, COLS, C), BF16),
            pltpu.VMEM((2, COLS, 3 * C), F32),
            pltpu.VMEM((3, 2, COLS, C), BF16),
            pltpu.VMEM((4, 2, COLS, C), BF16),
            pltpu.VMEM((2, 2 * COLS, 128), F32),
            pltpu.SemaphoreType.DMA((SENDS,)),
            pltpu.SemaphoreType.DMA((SENDS,)),
            pltpu.SemaphoreType.DMA((LOADS,)),
        ],
        compiler_params=pltpu.CompilerParams(
            collective_id=0, has_side_effects=True, vmem_limit_bytes=56 * 1024 * 1024
        ),
    )(
        latent, attn_gain, qkv_weight, proj_weight, conv_gain, conv_weight, conv_bias, time_weight, time_bias,
        jnp.swapaxes(up_weight, 2, 3), up_bias,
    )


def solution(mesh):
    return jax.shard_map(
        body,
        mesh=mesh,
        in_specs=(P("tm", "space", None, None), P(), P(), P(), P(), P(), P(), P(), P(), P(), P()),
        out_specs=P("tm", "space", None, None),
        check_vma=False,
    )
```

```python
import math

import jax
import jax.numpy as jnp
from jax import lax
from jax.experimental import pallas as pl
from jax.experimental.pallas import tpu as pltpu
from jax.sharding import PartitionSpec as P

MESH = pl.DeviceIdType.MESH
F32 = jnp.float32
BF16 = jnp.bfloat16
C = 384
COLS = 160
NT = (((1,), (1,)), ((), ()))
PARTS = 4
PART = 80
OWN = PARTS * PART
HALF = 80
SIDES = (0, 3, 1, 2)
TIMES = (0, 2, 1)
ORDER = (
    ("own", 0), ("own", 1), ("f+", 0), ("f-", 0), ("own", 2), ("f-", 1), ("g+", 1, 0), ("own", 3), ("op", 0),
    ("query", 0), ("f+", 1), ("g+", 0, 1), ("g+", 0, 0), ("g+", 0, 3), ("g-", 1, 1), ("op", 1), ("attend", 0, 0, 1),
    ("g-", 0, 3), ("g-", 0, 0), ("g-", 0, 1), ("f+", 2), ("g+", 3, 0), ("g-", 1, 0), ("g-", 2, 0), ("g+", 0, 2),
    ("f-", 3), ("g-", 0, 2), ("attend", 0, 1, 2), ("table", 0), ("g-", 1, 2), ("g-", 1, 3), ("g+", 1, 1),
    ("go", 0, 0), ("g+", 1, 3), ("f-", 2), ("g+", 1, 2), ("attend", 1, 1, 2), ("go", 0, 3), ("g+", 2, 3), ("op", 2),
    ("go", 0, 1), ("g-", 3, 0), ("g+", 2, 0), ("f+", 3), ("go", 0, 2), ("attend", 0, 3, 2), ("op", 3), ("go", 1, 0),
    ("g+", 3, 1), ("g-", 2, 3), ("g-", 3, 1), ("go", 1, 1), ("go", 1, 2), ("go", 1, 3), ("attend", 1, 3, 2),
    ("g+", 2, 2), ("g+", 2, 1), ("g-", 2, 1), ("g-", 2, 2), ("attend", 2, 1, 2), ("go", 2, 0), ("g+", 3, 3),
    ("g-", 3, 2), ("g-", 3, 3), ("g+", 3, 2), ("attend", 3, 1, 2), ("go", 3, 1), ("go", 2, 3), ("go", 2, 1),
    ("go", 2, 2), ("attend", 2, 3, 2), ("go", 3, 3), ("go", 3, 0), ("go", 3, 2),
)


def rms(x, gain):
    values = x.astype(F32)
    return values * lax.rsqrt(jnp.mean(values * values, axis=-1, keepdims=True) + 1e-06) * gain


def silu(x):
    return x / (1.0 + jnp.exp(-x))


def dot(a, b):
    return jnp.dot(a, b, preferred_element_type=F32)


def flat(x):
    return x.reshape(-1, x.shape[-1])


def moved(x, steps):
    index = lax.broadcasted_iota(jnp.int32, x.shape, 0)
    edge = 0 if steps == 1 else COLS - 1
    rolled = pltpu.roll(x, steps % x.shape[0], 0)
    keep = index != edge
    for run in range(1, x.shape[0] // COLS):
        keep = keep & (index != edge + run * COLS)
    return jnp.where(keep, rolled, 0.0)


def kernel(
    latent, attn_gain_hbm, qkv_hbm, proj_hbm, conv_gain_hbm, conv_hbm, conv_bias_hbm, time_hbm, time_bias_hbm, up_hbm,
    up_bias_hbm, out_hbm,
    attn_gain, conv_gain, conv_bias, time_bias, up_bias, out,
    lat, nb, qb, acc, mx, den, acc_out, stat_out, acc_in, stat_in,
    qkv, proj, wc, wt, up, wu,
    mid, mid_in, act, conv, blocks, frames, wide,
    ss, rs, ws,
):
    z = lax.axis_index("tm")
    s = lax.axis_index("space")
    core = lax.rem(s, 2)
    x = lax.rem(s // 2, 4)
    y = s // 8
    pos1 = x + core * (y - x)
    pos2 = y + core * (x - y)
    step1 = 2 + 6 * core
    step2 = 8 - 6 * core

    def at(zz, ss_):
        return (zz, ss_)

    sib = at(z, s + 1 - 2 * core)
    far = at(z, lax.rem(s + 2 * core + 31, 32))
    f_plus = at(z, s + (lax.rem(pos1 + 1, 4) - pos1) * step1)
    f_minus = at(z, s + (lax.rem(pos1 + 3, 4) - pos1) * step1)
    g_plus = at(z, s + (lax.rem(pos2 + 1, 4) - pos2) * step2)
    g_minus = at(z, s + (lax.rem(pos2 + 3, 4) - pos2) * step2)
    z_plus = at(lax.rem(z + 1, 8), s)
    z_minus = at(lax.rem(z + 7, 8), s)
    z_plus2 = at(lax.rem(z + 2, 8), s)
    z_minus2 = at(lax.rem(z + 6, 8), s)

    pending = []
    local = []

    def send(src, dst, device):
        k = len(pending)
        copy = pltpu.make_async_remote_copy(
            src_ref=src, dst_ref=dst, send_sem=ss.at[k], recv_sem=rs.at[k], device_id=device, device_id_type=MESH
        )
        copy.start()
        pending.append(copy)
        return copy

    left = []

    def sent(*copies):
        for copy in copies:
            copy.wait_send()
            left.append(id(copy))


    def load(src, dst):
        copy = pltpu.make_async_copy(src, dst, ws.at[len(local)])
        copy.start()
        local.append(copy)
        return copy

    barrier = pltpu.get_barrier_semaphore()
    partners = (sib, far, f_plus, f_minus, g_plus, g_minus, z_plus, z_minus, z_plus2, z_minus2)
    for partner in partners:
        pl.semaphore_signal(barrier, inc=1, device_id=partner, device_id_type=MESH)
    gain_load = load(attn_gain_hbm, attn_gain)
    qkv_load = load(qkv_hbm, qkv)
    pl.semaphore_wait(barrier, len(partners))

    shift = []

    def shift_next():
        c = len(shift)
        if c < PARTS:
            if c:
                sent(shift[-1])
            shift.append(send(latent.at[0, c // 2, pl.ds(c % 2 * PART, PART)], lat.at[c], z_plus2))

    shift_next()
    proj_load = load(proj_hbm, proj)
    conv_loads = [
        [load(conv_hbm.at[dt, :, dx], wc.at[TIMES.index(dt), :, :, pl.ds(dx * C, C)]) for dx in range(3)]
        for dt in TIMES
    ]
    time_loads = [load(time_hbm.at[dt], wt.at[TIMES.index(dt)]) for dt in TIMES]
    up_load = load(up_hbm, up)
    small_loads = [
        load(conv_gain_hbm, conv_gain),
        load(conv_bias_hbm, conv_bias),
        load(time_bias_hbm, time_bias),
        load(up_bias_hbm, up_bias),
    ]

    mx[...] = jnp.full(mx.shape, -1e30, F32)
    den[...] = jnp.zeros(den.shape, F32)
    acc[...] = jnp.zeros(acc.shape, F32)

    copies = {}

    def slot(c, j, i):
        return nb.at[4 * c + SIDES.index(j), i]

    def along_second(c, i):
        copies["g+", c, i] = send(slot(c, 0, i), slot(c, 3, i), g_plus)
        copies["g-", c, i] = send(slot(c, 0, i), slot(c, 1, i), g_minus)

    def step(kind, c, i=0):
        if kind == "own":
            shift[c].wait_recv()
            nb[4 * c, 0] = rms(lat[c], attn_gain[...].reshape(1, C)).astype(BF16)
            copies["f+", c, 0] = send(slot(c, 0, 0), slot(c, 0, 3), f_plus)
            copies["f-", c, 0] = send(slot(c, 0, 0), slot(c, 0, 1), f_minus)
            along_second(c, 0)
            shift_next()
            return
        copies[kind, c, i].wait_recv()
        if kind == "f+":
            if c % 2 == 0:
                copies["op", c, 0] = send(slot(c, 0, 3), slot(c, 0, 2), f_plus)
            along_second(c, 3)
        elif kind == "f-":
            if c % 2 == 1:
                copies["op", c, 0] = send(slot(c, 0, 1), slot(c, 0, 2), f_minus)
            along_second(c, 1)
        elif kind == "op":
            along_second(c, 2)
        elif kind == "g+" and (c + i) % 2 == 0:
            copies["go", c, i] = send(slot(c, 3, i), slot(c, 2, i), g_plus)
        elif kind == "g-" and (c + i) % 2 == 1:
            copies["go", c, i] = send(slot(c, 1, i), slot(c, 2, i), g_minus)

    def project():
        qkv_load.wait()
        scale = math.log2(math.e) / math.sqrt(C)
        normed = jnp.concatenate([nb[4 * c, 0] for c in range(PARTS)], axis=0)
        query = dot(normed, qkv[:, :C]).astype(BF16)
        query = lax.dot_general(query, qkv[:, C : 2 * C], NT, preferred_element_type=F32) * scale
        qb[:OWN] = query.astype(BF16)
        return send(qb.at[pl.ds(0, OWN)], qb.at[pl.ds(OWN, OWN)], sib)

    def attend(c, p, n, low=0, size=2 * OWN):
        rows = slice(low, low + size)
        count = n * OWN
        keys = nb[4 * c + p : 4 * c + p + n].reshape(count, C)
        scores = lax.dot_general(qb[rows], keys, NT, preferred_element_type=F32)
        top = mx[rows]
        new_top = jnp.maximum(top, jnp.max(scores, axis=1, keepdims=True))
        expo = jnp.exp2(scores - jnp.tile(new_top, (1, -(-count // 128)))[:, :count])
        fade = jnp.exp2(top - new_top)
        if count % 128 == 0:
            part = expo[:, :128]
            for lane in range(128, count, 128):
                part = part + expo[:, lane : lane + 128]
        else:
            part = jnp.sum(expo, axis=1, keepdims=True) * (1.0 / 128.0)
        mx[rows] = new_top
        den[rows] = den[rows] * fade + part
        acc[rows] = acc[rows] * jnp.tile(fade, (1, C // 128)) + dot(expo.astype(BF16), keys)

    def table():
        def summed(parts):
            return parts[0] if len(parts) == 1 else parts[0] + parts[1]

        spans = {(0, 0): (0,), (0, 1): (1, 2), (1, 0): (0, 1), (1, 1): (2,)}
        for a in range(2):
            for e in range(2):
                rows = [summed([up[dy, dx].astype(F32) for dy in spans[a, e]]) for dx in range(3)]
                for k, (b, f) in enumerate(((0, 1), (1, 0), (0, 0), (1, 1))):
                    cell = summed([rows[dx] for dx in spans[b, f]]).astype(BF16)
                    wu[a, k * C // 2 : (k + 1) * C // 2, e * C : (e + 1) * C] = cell

    gain_load.wait()
    for _ in range(SHIFT_AHEAD):
        shift_next()
    for kind, c, *rest in ORDER:
        if kind == "query":
            q_copy = project()
        elif kind == "attend":
            if q_copy is not None:
                q_copy = q_copy.wait_recv()
            attend(c, *rest)
        elif kind == "table":
            up_load.wait()
            table()
        else:
            step(kind, c, *rest)
    attend(PARTS - 1, 3, 1, OWN, OWN)
    acc_out[...] = acc[OWN:].astype(BF16)
    lane = lax.broadcasted_iota(jnp.int32, (OWN, 128), 1)
    stat_out[...] = jnp.where(lane < 64, mx[OWN:], jnp.sum(den[OWN:], axis=1, keepdims=True))
    back = [send(acc_out, acc_in, sib), send(stat_out, stat_in, sib)]
    attend(PARTS - 1, 3, 1, 0, OWN)
    for copy in [proj_load] + small_loads:
        copy.wait()
    for copy in back:
        copy.wait_recv()
    top = jnp.maximum(mx[:OWN, :1], stat_in[:, :1])
    mine = jnp.exp2(mx[:OWN, :1] - top)
    other = jnp.exp2(stat_in[:, :1] - top)
    total = jnp.sum(den[:OWN], axis=1, keepdims=True) * mine + stat_in[:, 64:65] * other
    pooled = (acc[:OWN] * (mine / total) + acc_in[...].astype(F32) * (other / total)).astype(BF16)
    attn = dot(pooled, qkv[:, 2 * C :]).astype(BF16)
    value = (flat(lat[...]).astype(F32) + dot(attn, proj[...])).astype(BF16)
    mid[...] = value.reshape(2, COLS, C)
    act[1, 1:3] = silu(rms(value, conv_gain[...].reshape(1, C))).astype(BF16).reshape(2, COLS, C)


    far_own, near_own = 1 + core, 2 - core
    far_halo, near_halo = 3 * core, 3 - 3 * core
    edge = lax.rem(s, 31) == 0

    def to_far(buffer):
        return send(buffer.at[far_own], buffer.at[near_halo], far)

    def to_near(buffer):
        return send(buffer.at[near_own], buffer.at[far_halo], sib)

    def halves():
        return [pl.ds(0, HALF), pl.ds(HALF, HALF)]

    def beside(own, run):
        return (
            send(act.at[1, own, run], act.at[0, own, run], z_plus),
            send(mid.at[own - 1, run], mid_in.at[own - 1, run], z_minus),
        )

    def arrived(pair, own, run, halo, device):
        pair[0].wait_recv()
        older = send(act.at[0, own, run], act.at[0, halo, run], device)
        pair[1].wait_recv()
        act[2, own, run] = silu(rms(mid_in[own - 1, run], conv_gain[...].reshape(1, C))).astype(BF16)
        return older, send(act.at[2, own, run], act.at[2, halo, run], device)

    def close(f):
        @pl.when(edge)
        def _():
            act[f, far_halo] = jnp.zeros((COLS, C), BF16)

    def taps(f, own):
        return jnp.concatenate([act[f, own - 1 + dy] for dy in range(3)], axis=1)

    def convolve(own):
        older = taps(0, own)
        older = jnp.where((z != 1) & (z != 2), older, jnp.zeros_like(older))
        both = jnp.concatenate([older, taps(2, own)], axis=1)
        value = conv[own - 1] + dot(both, wc[0:2].reshape(6 * C, 3 * C))
        value = value[:, C : 2 * C] + moved(value[:, :C], 1) + moved(value[:, 2 * C :], -1)
        value = value + conv_bias[...].reshape(1, C) + mid_in[own - 1].astype(F32)
        blocks[1, own - 1] = value.astype(BF16)

    def spread(own, run):
        return (
            send(blocks.at[1, own - 1, run], blocks.at[0, own - 1, run], z_plus),
            send(blocks.at[1, own - 1, run], blocks.at[2, own - 1, run], z_minus),
        )

    def double(pair, own, run, halo, device):
        for copy in pair:
            copy.wait_recv()
        older = blocks[0, own - 1, run]
        older = jnp.where(z >= 2, older, jnp.zeros_like(older))
        both = jnp.concatenate([older, blocks[2, own - 1, run]], axis=1)
        value = (conv[own - 1, run, : 2 * C] + dot(both, wt[0:2].reshape(2 * C, 2 * C))).astype(BF16)
        frames[own, 0, run] = value[:, :C]
        frames[own, 1, run] = value[:, C:]
        return send(frames.at[own, :, run], frames.at[halo, :, run], device)

    bias = up_bias[...].reshape(1, C // 2)

    stores = []

    def upsample(i, a):
        rows = jnp.concatenate([flat(frames[i + a]), flat(frames[i + a + 1])], axis=1)
        value = lax.dot_general(rows, wu[a], NT, preferred_element_type=F32)
        side = value[:, C:]
        lane = lax.broadcasted_iota(jnp.int32, side.shape, 1)
        value = value[:, :C] + jnp.where(lane < C // 2, moved(side, 1), moved(side, -1))
        second = pltpu.roll(value, C // 2, 1)
        for frame in range(2):
            run = slice(frame * COLS, (frame + 1) * COLS)
            for part in range(2):
                lanes = slice(128 * part, 128 * part + 128)
                wide[part, pl.ds(0, COLS, stride=2), :] = value[run, lanes]
                wide[part, pl.ds(1, COLS, stride=2), :] = second[run, lanes]
            out[frame, 2 * i + a, :, :128] = (wide[0] + bias[:, :128]).astype(BF16)
            out[frame, 2 * i + a, :, 128:] = (wide[1, :, : C // 2 - 128] + bias[:, 128:]).astype(BF16)
        stores.append(load(out.at[:, 2 * i + a], out_hbm.at[:, 2 * i + a]))

    whole = pl.ds(0, COLS)
    far_pairs = [beside(far_own, run) for run in halves()]
    own_edges = to_far(act.at[1]), to_near(act.at[1])
    near_pair = beside(near_own, whole)
    for row in conv_loads:
        for copy in row:
            copy.wait()
    for copy in own_edges:
        copy.wait_recv()
    close(1)

    @pl.when(z != 1)
    def _():
        rows = jnp.concatenate([flat(act[1, dy : dy + 2]) for dy in range(3)], axis=1)
        conv[...] = dot(rows, wc[2].reshape(3 * C, 3 * C)).reshape(conv.shape)

    @pl.when(z == 1)
    def _():
        conv[...] = jnp.zeros(conv.shape, F32)

    far_edges = []
    for pair, run in zip(far_pairs, halves()):
        far_edges += arrived(pair, far_own, run, near_halo, far)
    near_edges = arrived(near_pair, near_own, whole, far_halo, sib)
    for copy in near_edges:
        copy.wait_recv()
    convolve(near_own)
    near_pair = spread(near_own, halves()[0])
    for copy in far_edges:
        copy.wait_recv()
    close(0)
    close(2)
    convolve(far_own)
    far_pairs = [spread(far_own, run) for run in halves()]
    for copy in time_loads:
        copy.wait()
    rows = flat(blocks[1])
    rows = jnp.where(z >= 1, rows, jnp.zeros_like(rows))
    near_pairs = [near_pair, spread(near_own, halves()[1])]
    conv[:, :, : 2 * C] = (dot(rows, wt[2]) + time_bias[...].reshape(1, 2 * C)).reshape(2, COLS, 2 * C)
    far_edges = [double(pair, far_own, run, near_halo, far) for pair, run in zip(far_pairs, halves())]
    near_edges = [double(pair, near_own, run, far_halo, sib) for pair, run in zip(near_pairs, halves())]
    upsample(0, 1)
    upsample(1, 0)
    for copy in near_edges:
        copy.wait_recv()
    upsample(1 - core, 1 - core)
    for copy in far_edges:
        copy.wait_recv()

    @pl.when(edge)
    def _():
        frames[far_halo] = jnp.zeros((2, COLS, C), BF16)

    upsample(core, core)
    for copy in pending:
        if id(copy) not in left:
            copy.wait_send()
    for copy in stores:
        copy.wait()


SHIFT_AHEAD = 2
SENDS = 96
LOADS = 32


def body(
    latent, attn_gain, qkv_weight, proj_weight, conv_gain, conv_weight, conv_bias, time_weight, time_bias, up_weight,
    up_bias,
):
    anywhere = pl.BlockSpec(memory_space=pl.ANY)
    return pl.pallas_call(
        kernel,
        out_shape=jax.ShapeDtypeStruct((2, 4, 2 * COLS, C // 2), BF16),
        in_specs=[anywhere] * 11,
        out_specs=anywhere,
        scratch_shapes=[
            pltpu.VMEM((C,), F32),
            pltpu.VMEM((C,), F32),
            pltpu.VMEM((C,), F32),
            pltpu.VMEM((2 * C,), F32),
            pltpu.VMEM((C // 2,), F32),
            pltpu.VMEM((2, 4, 2 * COLS, C // 2), BF16),
            pltpu.VMEM((PARTS, PART, C), BF16),
            pltpu.VMEM((4 * PARTS, 4, PART, C), BF16),
            pltpu.VMEM((2 * OWN, C), BF16),
            pltpu.VMEM((2 * OWN, C), F32),
            pltpu.VMEM((2 * OWN, 128), F32),
            pltpu.VMEM((2 * OWN, 128), F32),
            pltpu.VMEM((OWN, C), BF16),
            pltpu.VMEM((OWN, 128), F32),
            pltpu.VMEM((OWN, C), BF16),
            pltpu.VMEM((OWN, 128), F32),
            pltpu.VMEM((C, 3 * C), BF16),
            pltpu.VMEM((C, C), BF16),
            pltpu.VMEM((3, 3, C, 3 * C), BF16),
            pltpu.VMEM((3, C, 2 * C), BF16),
            pltpu.VMEM((3, 3, C // 2, C), BF16),
            pltpu.VMEM((2, 2 * C, 2 * C), BF16),
            pltpu.VMEM((2, COLS, C), BF16),
            pltpu.VMEM((2, COLS, C), BF16),
            pltpu.VMEM((3, 4, COLS, C), BF16),
            pltpu.VMEM((2, COLS, 3 * C), F32),
            pltpu.VMEM((3, 2, COLS, C), BF16),
            pltpu.VMEM((4, 2, COLS, C), BF16),
            pltpu.VMEM((2, 2 * COLS, 128), F32),
            pltpu.SemaphoreType.DMA((SENDS,)),
            pltpu.SemaphoreType.DMA((SENDS,)),
            pltpu.SemaphoreType.DMA((LOADS,)),
        ],
        compiler_params=pltpu.CompilerParams(
            collective_id=0, has_side_effects=True, vmem_limit_bytes=56 * 1024 * 1024
        ),
    )(
        latent, attn_gain, qkv_weight, proj_weight, conv_gain, conv_weight, conv_bias, time_weight, time_bias,
        jnp.swapaxes(up_weight, 2, 3), up_bias,
    )


def solution(mesh):
    return jax.shard_map(
        body,
        mesh=mesh,
        in_specs=(P("tm", "space", None, None), P(), P(), P(), P(), P(), P(), P(), P(), P(), P()),
        out_specs=P("tm", "space", None, None),
        check_vma=False,
    )
```

```python
import math

import jax
import jax.numpy as jnp
from jax import lax
from jax.experimental import pallas as pl
from jax.experimental.pallas import tpu as pltpu
from jax.sharding import PartitionSpec as P

MESH = pl.DeviceIdType.MESH
F32 = jnp.float32
BF16 = jnp.bfloat16
C = 384
COLS = 160
NT = (((1,), (1,)), ((), ()))
PARTS = 4
PART = 80
OWN = PARTS * PART
HALF = 80
SIDES = (0, 3, 1, 2)
TIMES = (0, 2, 1)
ORDER = (
    ("own", 0), ("own", 1), ("f+", 0), ("g-", 0, 0), ("f-", 0), ("own", 2), ("f-", 1), ("own", 3), ("op", 0),
    ("g+", 1, 0), ("g-", 2, 0), ("f+", 1), ("op", 1), ("g+", 0, 1), ("g+", 0, 3), ("f+", 2), ("query", 0),
    ("g-", 0, 3), ("g-", 0, 1), ("attend", 0, 0, 1), ("g+", 0, 0), ("g-", 1, 1), ("g-", 1, 0), ("g+", 3, 0),
    ("g-", 0, 2), ("g+", 0, 2), ("f-", 3), ("attend", 0, 1, 2), ("table", 0), ("g+", 1, 3), ("g-", 1, 3),
    ("g+", 1, 1), ("g-", 1, 2), ("g+", 1, 2), ("op", 2), ("attend", 1, 1, 2), ("f-", 2), ("go", 0, 0), ("go", 0, 3),
    ("g+", 2, 0), ("g-", 3, 0), ("go", 0, 1), ("f+", 3), ("go", 0, 2), ("attend", 0, 3, 2), ("go", 1, 0), ("op", 3),
    ("go", 1, 3), ("g-", 2, 3), ("g-", 3, 1), ("g+", 2, 3), ("go", 1, 2), ("g+", 3, 1), ("go", 1, 1),
    ("attend", 1, 3, 2), ("g-", 2, 1), ("g+", 2, 1), ("g-", 2, 2), ("g+", 2, 2), ("attend", 2, 1, 2), ("g+", 3, 3),
    ("g-", 3, 3), ("g-", 3, 2), ("g+", 3, 2), ("go", 3, 0), ("attend", 3, 1, 2), ("go", 2, 3), ("go", 3, 1),
    ("go", 2, 0), ("go", 2, 1), ("go", 2, 2), ("attend", 2, 3, 2), ("go", 3, 3), ("go", 3, 2),
)


def rms(x, gain):
    values = x.astype(F32)
    return values * lax.rsqrt(jnp.mean(values * values, axis=-1, keepdims=True) + 1e-06) * gain


def silu(x):
    return x / (1.0 + jnp.exp(-x))


def dot(a, b):
    return jnp.dot(a, b, preferred_element_type=F32)


def flat(x):
    return x.reshape(-1, x.shape[-1])


def moved(x, steps):
    index = lax.broadcasted_iota(jnp.int32, x.shape, 0)
    edge = 0 if steps == 1 else COLS - 1
    rolled = pltpu.roll(x, steps % x.shape[0], 0)
    keep = index != edge
    for run in range(1, x.shape[0] // COLS):
        keep = keep & (index != edge + run * COLS)
    return jnp.where(keep, rolled, 0.0)


def kernel(
    latent, attn_gain_hbm, qkv_hbm, proj_hbm, conv_gain_hbm, conv_hbm, conv_bias_hbm, time_hbm, time_bias_hbm, up_hbm,
    up_bias_hbm, out_hbm,
    attn_gain, conv_gain, conv_bias, time_bias, up_bias, out,
    lat, nb, qb, acc, mx, den, acc_out, stat_out, acc_in, stat_in,
    qkv, proj, wc, wt, up, wu,
    mid, mid_in, act, conv, blocks, frames, wide,
    ss, rs, ws,
):
    z = lax.axis_index("tm")
    s = lax.axis_index("space")
    core = lax.rem(s, 2)
    x = lax.rem(s // 2, 4)
    y = s // 8
    pos1 = x + core * (y - x)
    pos2 = y + core * (x - y)
    step1 = 2 + 6 * core
    step2 = 8 - 6 * core

    def at(zz, ss_):
        return (zz, ss_)

    sib = at(z, s + 1 - 2 * core)
    far = at(z, lax.rem(s + 2 * core + 31, 32))
    f_plus = at(z, s + (lax.rem(pos1 + 1, 4) - pos1) * step1)
    f_minus = at(z, s + (lax.rem(pos1 + 3, 4) - pos1) * step1)
    g_plus = at(z, s + (lax.rem(pos2 + 1, 4) - pos2) * step2)
    g_minus = at(z, s + (lax.rem(pos2 + 3, 4) - pos2) * step2)
    z_plus = at(lax.rem(z + 1, 8), s)
    z_minus = at(lax.rem(z + 7, 8), s)
    z_plus2 = at(lax.rem(z + 2, 8), s)
    z_minus2 = at(lax.rem(z + 6, 8), s)

    pending = []
    local = []

    def send(src, dst, device):
        k = len(pending)
        copy = pltpu.make_async_remote_copy(
            src_ref=src, dst_ref=dst, send_sem=ss.at[k], recv_sem=rs.at[k], device_id=device, device_id_type=MESH
        )
        copy.start()
        pending.append(copy)
        return copy

    left = []

    def sent(*copies):
        for copy in copies:
            copy.wait_send()
            left.append(id(copy))


    def load(src, dst):
        copy = pltpu.make_async_copy(src, dst, ws.at[len(local)])
        copy.start()
        local.append(copy)
        return copy

    barrier = pltpu.get_barrier_semaphore()
    partners = (sib, far, f_plus, f_minus, g_plus, g_minus, z_plus, z_minus, z_plus2, z_minus2)
    for partner in partners:
        pl.semaphore_signal(barrier, inc=1, device_id=partner, device_id_type=MESH)
    gain_load = load(attn_gain_hbm, attn_gain)
    qkv_load = load(qkv_hbm, qkv)
    pl.semaphore_wait(barrier, len(partners))

    shift = []

    def shift_next():
        c = len(shift)
        if c < PARTS:
            if c:
                sent(shift[-1])
            shift.append(send(latent.at[0, c // 2, pl.ds(c % 2 * PART, PART)], lat.at[c], z_plus2))

    shift_next()
    proj_load = load(proj_hbm, proj)
    conv_loads = [
        [load(conv_hbm.at[dt, :, dx], wc.at[TIMES.index(dt), :, :, pl.ds(dx * C, C)]) for dx in range(3)]
        for dt in TIMES
    ]
    time_loads = [load(time_hbm.at[dt], wt.at[TIMES.index(dt)]) for dt in TIMES]
    up_load = load(up_hbm, up)
    small_loads = [
        load(conv_gain_hbm, conv_gain),
        load(conv_bias_hbm, conv_bias),
        load(time_bias_hbm, time_bias),
        load(up_bias_hbm, up_bias),
    ]

    mx[...] = jnp.full(mx.shape, -1e30, F32)
    den[...] = jnp.zeros(den.shape, F32)
    acc[...] = jnp.zeros(acc.shape, F32)

    copies = {}

    def slot(c, j, i):
        return nb.at[4 * c + SIDES.index(j), i]

    def along_second(c, i):
        copies["g+", c, i] = send(slot(c, 0, i), slot(c, 3, i), g_plus)
        copies["g-", c, i] = send(slot(c, 0, i), slot(c, 1, i), g_minus)

    def step(kind, c, i=0):
        if kind == "own":
            shift[c].wait_recv()
            nb[4 * c, 0] = rms(lat[c], attn_gain[...].reshape(1, C)).astype(BF16)
            copies["f+", c, 0] = send(slot(c, 0, 0), slot(c, 0, 3), f_plus)
            copies["f-", c, 0] = send(slot(c, 0, 0), slot(c, 0, 1), f_minus)
            along_second(c, 0)
            shift_next()
            return
        copies[kind, c, i].wait_recv()
        if kind == "f+":
            if c % 2 == 0:
                copies["op", c, 0] = send(slot(c, 0, 3), slot(c, 0, 2), f_plus)
            along_second(c, 3)
        elif kind == "f-":
            if c % 2 == 1:
                copies["op", c, 0] = send(slot(c, 0, 1), slot(c, 0, 2), f_minus)
            along_second(c, 1)
        elif kind == "op":
            along_second(c, 2)
        elif kind == "g+" and (c + i) % 2 == 0:
            copies["go", c, i] = send(slot(c, 3, i), slot(c, 2, i), g_plus)
        elif kind == "g-" and (c + i) % 2 == 1:
            copies["go", c, i] = send(slot(c, 1, i), slot(c, 2, i), g_minus)

    def project():
        qkv_load.wait()
        scale = math.log2(math.e) / math.sqrt(C)
        normed = jnp.concatenate([nb[4 * c, 0] for c in range(PARTS)], axis=0)
        query = dot(normed, qkv[:, :C]).astype(BF16)
        query = lax.dot_general(query, qkv[:, C : 2 * C], NT, preferred_element_type=F32) * scale
        qb[:OWN] = query.astype(BF16)
        return send(qb.at[pl.ds(0, OWN)], qb.at[pl.ds(OWN, OWN)], sib)

    def attend(c, p, n, low=0, size=2 * OWN):
        rows = slice(low, low + size)
        count = n * OWN
        keys = nb[4 * c + p : 4 * c + p + n].reshape(count, C)
        scores = lax.dot_general(qb[rows], keys, NT, preferred_element_type=F32)
        top = mx[rows]
        new_top = jnp.maximum(top, jnp.max(scores, axis=1, keepdims=True))
        expo = jnp.exp2(scores - jnp.tile(new_top, (1, -(-count // 128)))[:, :count])
        fade = jnp.exp2(top - new_top)
        if count % 128 == 0:
            part = expo[:, :128]
            for lane in range(128, count, 128):
                part = part + expo[:, lane : lane + 128]
        else:
            part = jnp.sum(expo, axis=1, keepdims=True) * (1.0 / 128.0)
        mx[rows] = new_top
        den[rows] = den[rows] * fade + part
        acc[rows] = acc[rows] * jnp.tile(fade, (1, C // 128)) + dot(expo.astype(BF16), keys)

    def table():
        def summed(parts):
            return parts[0] if len(parts) == 1 else parts[0] + parts[1]

        spans = {(0, 0): (0,), (0, 1): (1, 2), (1, 0): (0, 1), (1, 1): (2,)}
        for a in range(2):
            for e in range(2):
                rows = [summed([up[dy, dx].astype(F32) for dy in spans[a, e]]) for dx in range(3)]
                for k, (b, f) in enumerate(((0, 1), (1, 0), (0, 0), (1, 1))):
                    cell = summed([rows[dx] for dx in spans[b, f]]).astype(BF16)
                    wu[a, k * C // 2 : (k + 1) * C // 2, e * C : (e + 1) * C] = cell

    gain_load.wait()
    for _ in range(SHIFT_AHEAD):
        shift_next()
    for kind, c, *rest in ORDER:
        if kind == "query":
            q_copy = project()
        elif kind == "attend":
            if q_copy is not None:
                q_copy = q_copy.wait_recv()
            attend(c, *rest)
        elif kind == "table":
            up_load.wait()
            table()
        else:
            step(kind, c, *rest)
    attend(PARTS - 1, 3, 1, OWN, OWN)
    acc_out[...] = acc[OWN:].astype(BF16)
    lane = lax.broadcasted_iota(jnp.int32, (OWN, 128), 1)
    stat_out[...] = jnp.where(lane < 64, mx[OWN:], jnp.sum(den[OWN:], axis=1, keepdims=True))
    back = [send(acc_out, acc_in, sib), send(stat_out, stat_in, sib)]
    attend(PARTS - 1, 3, 1, 0, OWN)
    for copy in [proj_load] + small_loads:
        copy.wait()
    for copy in back:
        copy.wait_recv()
    top = jnp.maximum(mx[:OWN, :1], stat_in[:, :1])
    mine = jnp.exp2(mx[:OWN, :1] - top)
    other = jnp.exp2(stat_in[:, :1] - top)
    total = jnp.sum(den[:OWN], axis=1, keepdims=True) * mine + stat_in[:, 64:65] * other
    pooled = (acc[:OWN] * (mine / total) + acc_in[...].astype(F32) * (other / total)).astype(BF16)
    attn = dot(pooled, qkv[:, 2 * C :]).astype(BF16)
    value = (flat(lat[...]).astype(F32) + dot(attn, proj[...])).astype(BF16)
    mid[...] = value.reshape(2, COLS, C)
    act[1, 1:3] = silu(rms(value, conv_gain[...].reshape(1, C))).astype(BF16).reshape(2, COLS, C)


    far_own, near_own = 1 + core, 2 - core
    far_halo, near_halo = 3 * core, 3 - 3 * core
    edge = lax.rem(s, 31) == 0

    def to_far(buffer):
        return send(buffer.at[far_own], buffer.at[near_halo], far)

    def to_near(buffer):
        return send(buffer.at[near_own], buffer.at[far_halo], sib)

    def halves():
        return [pl.ds(0, HALF), pl.ds(HALF, HALF)]

    def beside(own, run):
        return (
            send(act.at[1, own, run], act.at[0, own, run], z_plus),
            send(mid.at[own - 1, run], mid_in.at[own - 1, run], z_minus),
        )

    def arrived(pair, own, run, halo, device):
        pair[0].wait_recv()
        older = send(act.at[0, own, run], act.at[0, halo, run], device)
        pair[1].wait_recv()
        act[2, own, run] = silu(rms(mid_in[own - 1, run], conv_gain[...].reshape(1, C))).astype(BF16)
        return older, send(act.at[2, own, run], act.at[2, halo, run], device)

    def close(f):
        @pl.when(edge)
        def _():
            act[f, far_halo] = jnp.zeros((COLS, C), BF16)

    def taps(f, own):
        return jnp.concatenate([act[f, own - 1 + dy] for dy in range(3)], axis=1)

    def convolve(own):
        older = taps(0, own)
        older = jnp.where((z != 1) & (z != 2), older, jnp.zeros_like(older))
        both = jnp.concatenate([older, taps(2, own)], axis=1)
        value = conv[own - 1] + dot(both, wc[0:2].reshape(6 * C, 3 * C))
        value = value[:, C : 2 * C] + moved(value[:, :C], 1) + moved(value[:, 2 * C :], -1)
        value = value + conv_bias[...].reshape(1, C) + mid_in[own - 1].astype(F32)
        blocks[1, own - 1] = value.astype(BF16)

    def spread(own, run):
        return (
            send(blocks.at[1, own - 1, run], blocks.at[0, own - 1, run], z_plus),
            send(blocks.at[1, own - 1, run], blocks.at[2, own - 1, run], z_minus),
        )

    def double(pair, own, run, halo, device):
        for copy in pair:
            copy.wait_recv()
        older = blocks[0, own - 1, run]
        older = jnp.where(z >= 2, older, jnp.zeros_like(older))
        both = jnp.concatenate([older, blocks[2, own - 1, run]], axis=1)
        value = (conv[own - 1, run, : 2 * C] + dot(both, wt[0:2].reshape(2 * C, 2 * C))).astype(BF16)
        frames[own, 0, run] = value[:, :C]
        frames[own, 1, run] = value[:, C:]
        return send(frames.at[own, :, run], frames.at[halo, :, run], device)

    bias = up_bias[...].reshape(1, C // 2)

    stores = []

    def upsample(i, a):
        rows = jnp.concatenate([flat(frames[i + a]), flat(frames[i + a + 1])], axis=1)
        value = lax.dot_general(rows, wu[a], NT, preferred_element_type=F32)
        side = value[:, C:]
        lane = lax.broadcasted_iota(jnp.int32, side.shape, 1)
        value = value[:, :C] + jnp.where(lane < C // 2, moved(side, 1), moved(side, -1))
        second = pltpu.roll(value, C // 2, 1)
        for frame in range(2):
            run = slice(frame * COLS, (frame + 1) * COLS)
            for part in range(2):
                lanes = slice(128 * part, 128 * part + 128)
                wide[part, pl.ds(0, COLS, stride=2), :] = value[run, lanes]
                wide[part, pl.ds(1, COLS, stride=2), :] = second[run, lanes]
            out[frame, 2 * i + a, :, :128] = (wide[0] + bias[:, :128]).astype(BF16)
            out[frame, 2 * i + a, :, 128:] = (wide[1, :, : C // 2 - 128] + bias[:, 128:]).astype(BF16)
        stores.append(load(out.at[:, 2 * i + a], out_hbm.at[:, 2 * i + a]))

    whole = pl.ds(0, COLS)
    far_pairs = [beside(far_own, run) for run in halves()]
    own_edges = to_far(act.at[1]), to_near(act.at[1])
    near_pair = beside(near_own, whole)
    for row in conv_loads:
        for copy in row:
            copy.wait()
    for copy in own_edges:
        copy.wait_recv()
    close(1)

    @pl.when(z != 1)
    def _():
        rows = jnp.concatenate([flat(act[1, dy : dy + 2]) for dy in range(3)], axis=1)
        conv[...] = dot(rows, wc[2].reshape(3 * C, 3 * C)).reshape(conv.shape)

    @pl.when(z == 1)
    def _():
        conv[...] = jnp.zeros(conv.shape, F32)

    far_edges = []
    for pair, run in zip(far_pairs, halves()):
        far_edges += arrived(pair, far_own, run, near_halo, far)
    near_edges = arrived(near_pair, near_own, whole, far_halo, sib)
    for copy in near_edges:
        copy.wait_recv()
    convolve(near_own)
    near_pair = spread(near_own, halves()[0])
    for copy in far_edges:
        copy.wait_recv()
    close(0)
    close(2)
    convolve(far_own)
    far_pairs = [spread(far_own, run) for run in halves()]
    for copy in time_loads:
        copy.wait()
    rows = flat(blocks[1])
    rows = jnp.where(z >= 1, rows, jnp.zeros_like(rows))
    near_pairs = [near_pair, spread(near_own, halves()[1])]
    conv[:, :, : 2 * C] = (dot(rows, wt[2]) + time_bias[...].reshape(1, 2 * C)).reshape(2, COLS, 2 * C)
    far_edges = [double(pair, far_own, run, near_halo, far) for pair, run in zip(far_pairs, halves())]
    near_edges = [double(pair, near_own, run, far_halo, sib) for pair, run in zip(near_pairs, halves())]
    upsample(0, 1)
    upsample(1, 0)
    for copy in near_edges:
        copy.wait_recv()
    upsample(1 - core, 1 - core)
    for copy in far_edges:
        copy.wait_recv()

    @pl.when(edge)
    def _():
        frames[far_halo] = jnp.zeros((2, COLS, C), BF16)

    upsample(core, core)
    for copy in pending:
        if id(copy) not in left:
            copy.wait_send()
    for copy in stores:
        copy.wait()


SHIFT_AHEAD = 2
SENDS = 96
LOADS = 32


def body(
    latent, attn_gain, qkv_weight, proj_weight, conv_gain, conv_weight, conv_bias, time_weight, time_bias, up_weight,
    up_bias,
):
    anywhere = pl.BlockSpec(memory_space=pl.ANY)
    return pl.pallas_call(
        kernel,
        out_shape=jax.ShapeDtypeStruct((2, 4, 2 * COLS, C // 2), BF16),
        in_specs=[anywhere] * 11,
        out_specs=anywhere,
        scratch_shapes=[
            pltpu.VMEM((C,), F32),
            pltpu.VMEM((C,), F32),
            pltpu.VMEM((C,), F32),
            pltpu.VMEM((2 * C,), F32),
            pltpu.VMEM((C // 2,), F32),
            pltpu.VMEM((2, 4, 2 * COLS, C // 2), BF16),
            pltpu.VMEM((PARTS, PART, C), BF16),
            pltpu.VMEM((4 * PARTS, 4, PART, C), BF16),
            pltpu.VMEM((2 * OWN, C), BF16),
            pltpu.VMEM((2 * OWN, C), F32),
            pltpu.VMEM((2 * OWN, 128), F32),
            pltpu.VMEM((2 * OWN, 128), F32),
            pltpu.VMEM((OWN, C), BF16),
            pltpu.VMEM((OWN, 128), F32),
            pltpu.VMEM((OWN, C), BF16),
            pltpu.VMEM((OWN, 128), F32),
            pltpu.VMEM((C, 3 * C), BF16),
            pltpu.VMEM((C, C), BF16),
            pltpu.VMEM((3, 3, C, 3 * C), BF16),
            pltpu.VMEM((3, C, 2 * C), BF16),
            pltpu.VMEM((3, 3, C // 2, C), BF16),
            pltpu.VMEM((2, 2 * C, 2 * C), BF16),
            pltpu.VMEM((2, COLS, C), BF16),
            pltpu.VMEM((2, COLS, C), BF16),
            pltpu.VMEM((3, 4, COLS, C), BF16),
            pltpu.VMEM((2, COLS, 3 * C), F32),
            pltpu.VMEM((3, 2, COLS, C), BF16),
            pltpu.VMEM((4, 2, COLS, C), BF16),
            pltpu.VMEM((2, 2 * COLS, 128), F32),
            pltpu.SemaphoreType.DMA((SENDS,)),
            pltpu.SemaphoreType.DMA((SENDS,)),
            pltpu.SemaphoreType.DMA((LOADS,)),
        ],
        compiler_params=pltpu.CompilerParams(
            collective_id=0, has_side_effects=True, vmem_limit_bytes=56 * 1024 * 1024
        ),
    )(
        latent, attn_gain, qkv_weight, proj_weight, conv_gain, conv_weight, conv_bias, time_weight, time_bias,
        jnp.swapaxes(up_weight, 2, 3), up_bias,
    )


def solution(mesh):
    return jax.shard_map(
        body,
        mesh=mesh,
        in_specs=(P("tm", "space", None, None), P(), P(), P(), P(), P(), P(), P(), P(), P(), P()),
        out_specs=P("tm", "space", None, None),
        check_vma=False,
    )
```
